128 devices in a mesh: seq: 64 (over y, z, x), dp: 2 (over core).
Axes of the slice: x: 4, y: 4, z: 4, core: 2. Of those that a mesh axis runs over, the one named last changes fastest.
Arguments:
- activation: bfloat16 [65536, 2048], P(('dp', 'seq')), parts along dimension 0, may hold values from -0.75 to 0.75
- step_size: float32 [65536, 32], P(('dp', 'seq')), parts along dimension 0, may hold values from 0 to 6, as said below
- decay_scale: float32 [64], P('dp'), parts along dimension 0, may hold values from -1 to 0
- write_vectors: bfloat16 [65536, 128], P(('dp', 'seq')), parts along dimension 0, may hold values from -3 to 3
- read_vectors: bfloat16 [65536, 128], P(('dp', 'seq')), parts along dimension 0, may hold values from -3 to 3
- upstream: bfloat16 [65536, 2048], P(('dp', 'seq')), parts along dimension 0, may hold values from -0.625 to 0.625
Outputs:
- activation_grad: bfloat16 [65536, 2048], P(('dp', 'seq')), parts along dimension 0
- logstep_grad: float32 [65536, 32], P(('dp', 'seq')), parts along dimension 0
- write_grad: float32 [65536, 128], P(('dp', 'seq')), parts along dimension 0
- readout_gradient: float32 [65536, 128], P(('dp', 'seq')), parts along dimension 0
The draws below stay inside these ranges and needn't reach their ends.
There are 2 independent parts, one for each index of `dp`. The reference program is written for one: setup_inputs(seed, part) draws one part's arguments, and reference() takes and returns one part's arrays. A program takes and returns all parts, laid end to end along the dimension named above; each array names one. Nothing has to cross between parts.
Inputs may be any that keep to these rules, and one draw needn't show every extreme that they name: `step_size`: step sizes are positive.
All inputs are finite; a program needn't handle non-finite values.
Results may differ from the reference program's by a relative error of at most 0.0055.
Values sent between devices are 32-bit elements; how exact they have to be, the bound alone decides.
No kernel may reach another device: no remote copies, remote signals or barrier semaphores. Data moves between devices by JAX's collectives and lax.ppermute only.
A program may use at most 384 MiB of HBM per device.

```python
import math
import jax
import jax.numpy as jnp
from jax import lax

HEADS = 32
HEAD_DIM = 64
STATE = 128
GROUP = 256
TOK_DEV = 512
TOKEN_POSITIONS = 32768
INNER = 2048


def head_laws(key):
    pick_key, rate_key = jax.random.split(jax.random.fold_in(key, 17), 2)
    share = 0.5
    pick = jax.random.uniform(pick_key, (HEADS,), jnp.float32)
    spread = jax.random.uniform(rate_key, (HEADS,), jnp.float32)
    slow_rate = jnp.exp(math.log(0.3 / TOKEN_POSITIONS) + spread * math.log(1.1 / 0.3))
    fast_low = math.log(1.0 / (2.0 * TOK_DEV))
    fast_rate = jnp.exp(fast_low + spread * (math.log(1.0 / 30.0) - fast_low))
    rate = jnp.where(pick < share, slow_rate, fast_rate)
    base = 0.5 * jnp.sqrt(30.0 * rate)
    return (rate, base)


def region_levels(key):
    quarter_key, device_key, group_key = jax.random.split(jax.random.fold_in(key, 43), 3)
    places = jnp.arange(TOKEN_POSITIONS, dtype=jnp.int32)
    quarter_log = jax.random.uniform(quarter_key, (4,), jnp.float32, -1.0, 0.0)
    device_log = jax.random.uniform(device_key, (TOKEN_POSITIONS // TOK_DEV,), jnp.float32, -1.0, 0.0)
    group_log = jax.random.uniform(group_key, (TOKEN_POSITIONS // GROUP,), jnp.float32, -0.5, 0.0)
    quarter_index = places * 4 // TOKEN_POSITIONS
    device_index = places // TOK_DEV
    group_index = places // GROUP
    level_log = quarter_log[quarter_index] + device_log[device_index] + group_log[group_index]
    return jnp.exp(level_log)


def draw_decay_scale(key, part):
    rate, base = head_laws(key)
    return (-(rate / base)).astype(jnp.float32)


def draw_step_size(key, part):
    rate, base = head_laws(key)
    coarse_random_key, spike_random_key = jax.random.split(jax.random.fold_in(key, 29), 2)
    rough = jnp.exp(jax.random.uniform(coarse_random_key, (TOKEN_POSITIONS, HEADS), jnp.float32, math.log(0.5), math.log(2.0)))
    sample_locations = jax.random.randint(spike_random_key, (4,), 0, TOKEN_POSITIONS)
    places = jnp.arange(TOKEN_POSITIONS, dtype=jnp.int32)
    struck = jnp.any(places[:, None] == sample_locations[None, :], axis=1)
    factor = jnp.where(struck, 6.0, 1.0)
    level = region_levels(key)
    return (base[None, :] * rough * (factor * level)[:, None]).astype(jnp.float32)


def shard_levels(rng, shape, cuts, smallest, high):
    gain = 1.0
    for dim, parts in cuts:
        draws = jax.random.uniform(jax.random.fold_in(jax.random.fold_in(rng, 6), dim), (parts,), jnp.float32, smallest / len(cuts), high / len(cuts))
        gain = gain * jnp.repeat(jnp.exp(draws), shape[dim] // parts).reshape((-1,) + (1,) * (len(shape) - 1 - dim))
    return gain


def centred(key, dims, scale, bound, shards=(), kind=jnp.bfloat16):
    level = shard_levels(key, dims, shards, -0.22, 0.18) if shards else 1.0
    entries = jax.random.normal(key, dims, jnp.float32) * scale * level
    return jnp.minimum(jnp.maximum(entries, -bound), bound).astype(kind)


def setup_inputs(seed: int = 0, part: int = 0) -> dict:
    seeds = jax.random.split(jax.random.key(seed), 7)
    part_splits = jax.random.split(jax.random.fold_in(seeds[6], part), 7)
    activation = centred(part_splits[0], (TOKEN_POSITIONS, INNER), 64 ** -0.5, 0.75, ((0, 64),))
    step_size = draw_step_size(jax.random.fold_in(jax.random.fold_in(seeds[6], part), 71), part)
    decay_scale = draw_decay_scale(jax.random.fold_in(jax.random.fold_in(seeds[6], part), 71), part)
    write_vectors = centred(part_splits[3], (TOKEN_POSITIONS, STATE), 4 ** -0.5, 3.0, ((0, 64),))
    read_vectors = centred(part_splits[4], (TOKEN_POSITIONS, STATE), 4 ** -0.5, 3.0, ((0, 64),))
    upstream = centred(part_splits[5], (TOKEN_POSITIONS, INNER), 100 ** -0.5, 0.625, ((0, 64),))
    return {"activation": activation, "step_size": step_size, "decay_scale": decay_scale, "write_vectors": write_vectors, "read_vectors": read_vectors, "upstream": upstream}


def group_states(blocks, decay_scale):
    activation, upstream, write_vectors, read_vectors, step_size = blocks
    row_count = activation.shape[0]
    head_count = decay_scale.shape[0]
    head_width = activation.shape[1] // head_count
    act_three = activation.astype(jnp.float32).reshape(row_count, head_count, head_width)
    up_three = upstream.astype(jnp.float32).reshape(row_count, head_count, head_width)
    log_decay = step_size * decay_scale[None, :]
    cumulative = jnp.cumsum(log_decay, axis=0)
    total_log = cumulative[-1]
    decay_in = jnp.exp(cumulative)
    decay_out = jnp.exp(total_log[None, :] - cumulative)
    act_scaled = (act_three * (step_size * decay_out)[:, :, None]).astype(jnp.bfloat16)
    up_scaled = (up_three * decay_in[:, :, None]).astype(jnp.bfloat16)
    state_part = jnp.einsum("sn,shp->hnp", write_vectors.astype(jnp.float32), act_scaled.astype(jnp.float32), precision=lax.Precision.HIGHEST)
    grad_part = jnp.einsum("un,uhp->hnp", read_vectors.astype(jnp.float32), up_scaled.astype(jnp.float32), precision=lax.Precision.HIGHEST)
    return act_scaled, up_scaled, state_part, grad_part, jnp.exp(total_log)


def group_full(blocks, enter_state, leave_grad, decay_scale):
    activation, upstream, write_vectors, read_vectors, step_size = blocks
    row_count = activation.shape[0]
    head_count = decay_scale.shape[0]
    head_width = activation.shape[1] // head_count
    high = lax.Precision.HIGHEST
    act_three = activation.astype(jnp.float32).reshape(row_count, head_count, head_width)
    up_three = upstream.astype(jnp.float32).reshape(row_count, head_count, head_width)
    write_wide = write_vectors.astype(jnp.float32)
    read_wide = read_vectors.astype(jnp.float32)
    log_decay = step_size * decay_scale[None, :]
    cumulative = jnp.cumsum(log_decay, axis=0)
    total_log = cumulative[-1]
    later_mask = lax.broadcasted_iota(jnp.int32, (row_count, row_count), 0) >= lax.broadcasted_iota(jnp.int32, (row_count, row_count), 1)
    gap_log = cumulative.T[:, :, None] - cumulative.T[:, None, :]
    decay_pairs = jnp.where(later_mask[None], jnp.exp(jnp.where(later_mask[None], gap_log, 0.0)), 0.0)
    pair_dots = jnp.einsum("thp,shp->hts", up_three, act_three, precision=high)
    scores = jnp.dot(read_vectors, write_vectors.T, preferred_element_type=jnp.float32)
    weighted = decay_pairs * pair_dots * step_size.T[:, None, :]
    coupled = scores[None] * weighted
    net_rows = jnp.sum(coupled, axis=2).T - jnp.sum(coupled, axis=1).T
    pair_sum = jnp.sum(weighted, axis=0).astype(jnp.bfloat16)
    write_part = jnp.dot(pair_sum.T, read_vectors, preferred_element_type=jnp.float32)
    read_part = jnp.dot(pair_sum, write_vectors, preferred_element_type=jnp.float32)
    masked = (decay_pairs * scores[None]).astype(jnp.bfloat16)
    back_local = jnp.einsum("hts,thp->shp", masked.astype(jnp.float32), up_three, precision=high)
    decay_in = jnp.exp(cumulative)
    decay_out = jnp.exp(total_log[None, :] - cumulative)
    act_scaled, up_scaled, state_part, grad_part, block_decay = group_states(blocks, decay_scale)
    leave_end = block_decay[:, None, None] * enter_state + state_part
    enter_low = enter_state.astype(jnp.bfloat16).astype(jnp.float32)
    leave_low = leave_grad.astype(jnp.bfloat16).astype(jnp.float32)
    offset = jnp.einsum("tn,hnp->thp", read_wide, enter_low, precision=high)
    row_cross = decay_in * jnp.sum(offset * up_three, axis=2)
    read_cross = jnp.einsum("thp,hnp->tn", up_scaled.astype(jnp.float32), enter_low, precision=high)
    back_cross = jnp.einsum("sn,hnp->shp", write_wide, leave_low, precision=high)
    back_total = back_local + decay_out[:, :, None] * back_cross
    write_cross = jnp.einsum("shp,hnp->sn", act_scaled.astype(jnp.float32), leave_low, precision=high)
    col_cross = step_size * decay_out * jnp.sum(act_three * back_cross, axis=2)
    net = net_rows + row_cross - col_cross
    boundary = jnp.sum(leave_grad * leave_end, axis=(1, 2))
    logarithm_gradient = jnp.flip(jnp.cumsum(jnp.flip(net, 0), axis=0), 0) + boundary[None, :]
    activation_grad = (step_size[:, :, None] * back_total).astype(jnp.bfloat16).reshape(row_count, head_count * head_width)
    logstep_grad = step_size * jnp.sum(act_three * back_total, axis=2) + log_decay * logarithm_gradient
    return activation_grad, logstep_grad, write_part + write_cross, read_part + read_cross


def reference(activation, step_size, decay_scale, write_vectors, read_vectors, upstream):
    total_rows, inner_width = activation.shape
    block_count = total_rows // GROUP
    blocks = (activation.reshape(block_count, GROUP, inner_width), upstream.reshape(block_count, GROUP, inner_width), write_vectors.reshape(block_count, GROUP, STATE), read_vectors.reshape(block_count, GROUP, STATE), step_size.reshape(block_count, GROUP, HEADS))
    zero_state = jnp.zeros((HEADS, STATE, HEAD_DIM), jnp.float32)

    def forward_step(carry_state, block_item):
        act_scaled, up_scaled, state_part, grad_part, block_decay = group_states(block_item, decay_scale)
        return block_decay[:, None, None] * carry_state + state_part, carry_state

    def backward_step(carry_grad, block_item):
        act_scaled, up_scaled, state_part, grad_part, block_decay = group_states(block_item, decay_scale)
        return grad_part + block_decay[:, None, None] * carry_grad, carry_grad

    last_state, enter_states = lax.scan(forward_step, zero_state, blocks)
    first_grad, leave_grads = lax.scan(backward_step, zero_state, blocks, reverse=True)

    def full_step(item):
        return group_full(item[0], item[1], item[2], decay_scale)

    activation_grad, logstep_grad, write_grad, readout_gradient = lax.map(full_step, (blocks, enter_states, leave_grads))
    return (activation_grad.reshape(total_rows, inner_width), logstep_grad.reshape(total_rows, HEADS), write_grad.reshape(total_rows, STATE), readout_gradient.reshape(total_rows, STATE))
```

```python
import math
from functools import partial

import jax
import jax.numpy as jnp
from jax import lax
from jax.experimental import pallas as pl
from jax.experimental.pallas import tpu as pltpu
from jax.sharding import PartitionSpec as P

GROUP = 256
LANES = 128
BUNCH = 8
LOG2E = math.log2(math.e)
F32 = jnp.float32
BF16 = jnp.bfloat16
MIB = 1 << 20


def dot_nn(a, b):
    return jnp.dot(a, b, preferred_element_type=F32)


def dot_nt(a, b):
    return lax.dot_general(a, b, (((1,), (1,)), ((), ())), preferred_element_type=F32)


def dot_tn(a, b):
    return lax.dot_general(a, b, (((0,), (0,)), ((), ())), preferred_element_type=F32)


def exact_dot(table, value):
    high = value.astype(BF16)
    rest = value - high.astype(F32)
    middle = rest.astype(BF16)
    low = (rest - middle.astype(F32)).astype(BF16)
    return dot_nn(table, high) + dot_nn(table, middle) + dot_nn(table, low)


def left_half(rows):
    return lax.broadcasted_iota(jnp.int32, (rows, LANES), 1) < LANES // 2


def pair_lanes(columns, pair):
    return jnp.where(
        left_half(columns.shape[0]),
        columns[:, 2 * pair : 2 * pair + 1],
        columns[:, 2 * pair + 1 : 2 * pair + 2],
    )


def order_table(size, upper):
    row = lax.broadcasted_iota(jnp.int32, (size, size), 0)
    column = lax.broadcasted_iota(jnp.int32, (size, size), 1)
    return jnp.where(row <= column if upper else row >= column, 1.0, 0.0)


def states_kernel(
    heads, piece_rows, dt_ref, scale_ref, write_ref, read_ref, act_ref, up_ref,
    pieces_ref, early_ref, late_ref, shifted_ref, out_ref, in_ref, across_ref, spread_ref,
    act_buf, up_buf, piece_buf, early_buf, late_buf, in_sems, out_sems,
):
    rows = dt_ref.shape[0]
    blocks = rows // GROUP
    bunches = heads // BUNCH
    wide = BUNCH // 2 * LANES
    loads = []
    for bunch in range(bunches):
        for which, (source, target) in enumerate(((act_ref, act_buf), (up_ref, up_buf))):
            lanes = pl.ds(bunch * wide, wide)
            copy = pltpu.make_async_copy(
                source.at[:, lanes], target.at[:, lanes], in_sems.at[bunch, which]
            )
            copy.start()
            loads.append(copy)
    table = order_table(GROUP, False).astype(BF16)
    decay_in, decay_out, totals = [], [], []
    for block in range(blocks):
        span = slice(block * GROUP, (block + 1) * GROUP)
        dt = dt_ref[span, :]
        running = exact_dot(table, dt * scale_ref[...])
        total = running[GROUP - 1 : GROUP, :]
        entering = jnp.exp(running)
        leaving = dt * jnp.exp(total - running)
        shifted = running * LOG2E - jnp.log2(dt)
        padded = jnp.concatenate(
            [running * LOG2E, jnp.zeros((GROUP, LANES - heads), F32)], axis=1
        )
        across = padded.T
        for bunch in range(bunches):
            few = slice(bunch * BUNCH, (bunch + 1) * BUNCH)
            shifted_ref[bunch, span, :] = shifted[:, few]
            out_ref[bunch, span, :] = leaving[:, few]
            in_ref[bunch, span, :] = entering[:, few]
            across_ref[bunch, :, span] = across[few, :]
        decay_in.append(entering)
        decay_out.append(leaving)
        totals.append(total)
    block_decay = [jnp.exp(total) for total in totals]
    device_decay = jnp.exp(totals[0] + totals[1])
    write_across = [write_ref[b * GROUP : (b + 1) * GROUP, :].T for b in range(blocks)]
    read_across = [read_ref[b * GROUP : (b + 1) * GROUP, :].T for b in range(blocks)]
    per_pair = LANES // piece_rows
    stores = []
    for bunch in range(bunches):
        lanes = slice(bunch * wide, (bunch + 1) * wide)
        loads[2 * bunch].wait()
        loads[2 * bunch + 1].wait()
        state, grad = [], []
        for block in range(blocks):
            span = slice(block * GROUP, (block + 1) * GROUP)
            act_scaled, up_scaled = [], []
            for pair in range(bunch * BUNCH // 2, (bunch + 1) * BUNCH // 2):
                here = slice(pair * LANES, (pair + 1) * LANES)
                act_scaled.append(
                    (act_buf[span, here].astype(F32) * pair_lanes(decay_out[block], pair)).astype(BF16)
                )
                up_scaled.append(
                    (up_buf[span, here].astype(F32) * pair_lanes(decay_in[block], pair)).astype(BF16)
                )
            state.append(dot_nn(write_across[block], jnp.concatenate(act_scaled, axis=1)))
            grad.append(dot_nn(read_across[block], jnp.concatenate(up_scaled, axis=1)))
        first, second, both = (
            jnp.concatenate(
                [pair_lanes(decay, pair) for pair in range(bunch * BUNCH // 2, (bunch + 1) * BUNCH // 2)],
                axis=1,
            )
            for decay in (block_decay[0], block_decay[1], device_decay)
        )
        spread_ref[:, lanes] = jnp.concatenate([first, second, both, jnp.zeros((5, wide), F32)], axis=0)
        device_state = second * state[0] + state[1]
        device_grad = grad[0] + first * grad[1]
        early_buf[:, lanes] = state[0]
        late_buf[:, lanes] = grad[1]
        for local in range(BUNCH // 2):
            pair = bunch * BUNCH // 2 + local
            here = slice(local * LANES, (local + 1) * LANES)
            few = slice(pair * per_pair, (pair + 1) * per_pair)
            piece_buf[few, :piece_rows, :] = device_state[:, here].reshape(per_pair, piece_rows, LANES)
            piece_buf[few, piece_rows : 2 * piece_rows, :] = device_grad[:, here].reshape(
                per_pair, piece_rows, LANES
            )
            piece_buf[few, 2 * piece_rows :, :] = jnp.broadcast_to(
                both[:, here][None], (per_pair, 8, LANES)
            )
        few = pl.ds(bunch * BUNCH // 2 * per_pair, BUNCH // 2 * per_pair)
        copies = (
            (piece_buf.at[few], pieces_ref.at[few]),
            (early_buf.at[:, pl.ds(bunch * wide, wide)], early_ref.at[:, pl.ds(bunch * wide, wide)]),
            (late_buf.at[:, pl.ds(bunch * wide, wide)], late_ref.at[:, pl.ds(bunch * wide, wide)]),
        )
        for which, (source, target) in enumerate(copies):
            copy = pltpu.make_async_copy(source, target, out_sems.at[bunch, which])
            copy.start()
            stores.append(copy)
    for copy in stores:
        copy.wait()


def scan_kernel(piece_rows, got_ref, carried_ref):
    count = got_ref.shape[0]
    zero = jnp.zeros((piece_rows, LANES), F32)

    def lap(step, carry):
        state, grad = carry
        carried_ref[step, :piece_rows, :] = state
        state = got_ref[step, 2 * piece_rows : 2 * piece_rows + 1, :] * state + got_ref[step, :piece_rows, :]
        back = count - 1 - step
        carried_ref[back, piece_rows:, :] = grad
        grad = (
            got_ref[back, piece_rows : 2 * piece_rows, :]
            + got_ref[back, 2 * piece_rows : 2 * piece_rows + 1, :] * grad
        )
        return state, grad

    lax.fori_loop(0, count, lap, (zero, zero), unroll=8)


def local_kernel(
    act_ref, up_ref, write_ref, read_ref, shifted_ref, across_ref,
    back_ref, rows_ref, write_part_ref, read_part_ref, pair_sum, scores,
):
    bunch = pl.program_id(1)
    half = GROUP // 2
    triangle = lax.broadcasted_iota(jnp.int32, (half, half), 0) <= lax.broadcasted_iota(
        jnp.int32, (half, half), 1
    )

    @pl.when(bunch == 0)
    def _():
        scores[...] = dot_nt(write_ref[...], read_ref[...])
        pair_sum[...] = jnp.zeros_like(pair_sum)

    left = left_half(GROUP)
    for pair in range(BUNCH // 2):
        here = slice(pair * LANES, (pair + 1) * LANES)
        act = act_ref[:, here]
        up = up_ref[:, here]
        back_top = jnp.zeros((half, LANES), F32)
        back_low = jnp.zeros((half, LANES), F32)
        for side in range(2):
            head = 2 * pair + side
            keep = left if side == 0 else jnp.logical_not(left)
            act_one = jnp.where(keep, act, jnp.zeros_like(act))
            up_one = jnp.where(keep, up, jnp.zeros_like(up))
            late = across_ref[0, head : head + 1, :]
            soon = shifted_ref[0, :, head : head + 1]
            decay_a = jnp.where(triangle, jnp.exp2(late[:, :half] - soon[:half]), 0.0)
            decay_b = jnp.exp2(late[:, half:] - soon[:half])
            decay_c = jnp.where(triangle, jnp.exp2(late[:, half:] - soon[half:]), 0.0)
            decay_top = jnp.concatenate([decay_a, decay_b], axis=1)
            dots_top = dot_nt(act_one[:half], up)
            dots_low = dot_nt(act_one[half:], up[half:])
            pair_sum[:half, :] += decay_top * dots_top
            pair_sum[half:, half:] += decay_c * dots_low
            masked_top = (decay_top * scores[:half, :]).astype(BF16)
            masked_low = (decay_c * scores[half:, half:]).astype(BF16)
            sums = jnp.sum(masked_top.astype(F32) * dots_top, axis=0, keepdims=True)
            low_sums = jnp.sum(masked_low.astype(F32) * dots_low, axis=0, keepdims=True)
            rows_ref[0, head : head + 1, :half] = sums[:, :half]
            rows_ref[0, head : head + 1, half:] = sums[:, half:] + low_sums
            back_top += dot_nn(masked_top, up_one)
            back_low += dot_nn(masked_low, up_one[half:])
        back_ref[:half, here] = back_top
        back_ref[half:, here] = back_low

    @pl.when(bunch == pl.num_programs(1) - 1)
    def _():
        low = pair_sum[...].astype(BF16)
        write_part_ref[...] = dot_nn(low, read_ref[...])
        read_part_ref[...] = dot_tn(low, write_ref[...])


def cross_kernel(
    heads, piece_rows, act_ref, up_ref, back_ref, carried_ref, pieces_ref, early_ref, late_ref,
    out_ref, in_ref, spread_ref, write_ref, read_ref, rows_ref, write_part_ref, read_part_ref, dt_ref, scale_ref,
    act_grad_ref, log_ref, write_grad_ref, read_grad_ref, row_acc, col_acc, edge_acc,
):
    bunch = pl.program_id(0)
    rows = act_ref.shape[0]
    per_pair = LANES // piece_rows

    @pl.when(bunch == 0)
    def _():
        row_acc[...] = jnp.zeros_like(row_acc)
        col_acc[...] = jnp.zeros_like(col_acc)
        edge_acc[...] = jnp.zeros_like(edge_acc)
        write_grad_ref[...] = write_part_ref[...]
        read_grad_ref[...] = read_part_ref[...]

    left = left_half(GROUP)
    lane = lax.broadcasted_iota(jnp.int32, (GROUP, LANES), 1)
    enters, leaves = [[], []], [[], []]
    edges = [edge_acc[0:1, :], edge_acc[1:2, :]]
    lane_one = lax.broadcasted_iota(jnp.int32, (1, LANES), 1)
    for pair in range(BUNCH // 2):
        here = slice(pair * LANES, (pair + 1) * LANES)
        few = slice(pair * per_pair, (pair + 1) * per_pair)
        enter_0 = carried_ref[few, :piece_rows, :].reshape(LANES, LANES)
        leave_1 = carried_ref[few, piece_rows:, :].reshape(LANES, LANES)
        own = pieces_ref[few, :piece_rows, :].reshape(LANES, LANES)
        enter_1 = spread_ref[0:1, here] * enter_0 + early_ref[:, here]
        leave_0 = late_ref[:, here] + spread_ref[1:2, here] * leave_1
        end_1 = spread_ref[2:3, here] * enter_0 + own
        enters[0].append(enter_0.astype(BF16))
        enters[1].append(enter_1.astype(BF16))
        leaves[0].append(leave_0.astype(BF16))
        leaves[1].append(leave_1.astype(BF16))
        for block, product in enumerate((leave_0 * enter_1, leave_1 * end_1)):
            sums = jnp.sum(product, axis=0, keepdims=True)
            for side in range(2):
                keep = left[:1] if side == 0 else jnp.logical_not(left[:1])
                one = jnp.sum(jnp.where(keep, sums, 0.0), axis=1, keepdims=True)
                edges[block] = jnp.where(lane_one == bunch * BUNCH + 2 * pair + side, one, edges[block])
    edge_acc[0:1, :] = edges[0]
    edge_acc[1:2, :] = edges[1]
    for block in range(rows // GROUP):
        span = slice(block * GROUP, (block + 1) * GROUP)
        enter_low = jnp.concatenate(enters[block], axis=1)
        leave_low = jnp.concatenate(leaves[block], axis=1)
        offset = dot_nn(read_ref[span, :], enter_low)
        cross = dot_nn(write_ref[span, :], leave_low)
        act_scaled, up_scaled = [], []
        row_sums, col_sums = row_acc[span, :], col_acc[span, :]
        for pair in range(BUNCH // 2):
            here = slice(pair * LANES, (pair + 1) * LANES)
            act = act_ref[span, here].astype(F32)
            decay_out = pair_lanes(out_ref[0, span, :], pair)
            up_one = up_ref[span, here].astype(F32) * pair_lanes(in_ref[0, span, :], pair)
            up_scaled.append(up_one.astype(BF16))
            act_scaled.append((act * decay_out).astype(BF16))
            total = back_ref[span, here] + decay_out * cross[:, here]
            act_grad_ref[span, here] = total.astype(BF16)
            row_product = offset[:, here] * up_one
            col_product = act * total
            for side in range(2):
                keep = left if side == 0 else jnp.logical_not(left)
                place = lane == bunch * BUNCH + 2 * pair + side
                row_sums = jnp.where(
                    place, jnp.sum(jnp.where(keep, row_product, 0.0), axis=1, keepdims=True), row_sums
                )
                col_sums = jnp.where(
                    place, jnp.sum(jnp.where(keep, col_product, 0.0), axis=1, keepdims=True), col_sums
                )
        row_acc[span, :] = row_sums
        col_acc[span, :] = col_sums
        read_grad_ref[span, :] += dot_nt(jnp.concatenate(up_scaled, axis=1), enter_low)
        write_grad_ref[span, :] += dot_nt(jnp.concatenate(act_scaled, axis=1), leave_low)

    @pl.when(bunch == pl.num_programs(0) - 1)
    def _():
        table = order_table(GROUP, True).astype(BF16)
        for block in range(rows // GROUP):
            span = slice(block * GROUP, (block + 1) * GROUP)
            local_rows = rows_ref[:, :, span].reshape(heads, GROUP)
            padded = jnp.concatenate([local_rows, jnp.zeros((LANES - heads, GROUP), F32)], axis=0).T
            net = (padded + row_acc[span, :] - col_acc[span, :])[:, :heads]
            log_grad = exact_dot(table, net) + edge_acc[block : block + 1, :heads]
            decay = dt_ref[span, :] * scale_ref[...]
            log_ref[span, :] = col_acc[span, :heads] + decay * log_grad


def on_device(activation, step_size, decay_scale, write_vectors, read_vectors, upstream):
    rows, inner = activation.shape
    heads = decay_scale.shape[0]
    state = write_vectors.shape[1]
    count = lax.axis_size("seq")
    pairs = heads // 2
    piece_rows = pairs * state // count
    bunches = heads // BUNCH
    blocks = rows // GROUP
    wide = inner // bunches
    scale = decay_scale.reshape(1, heads)
    vmem = pl.BlockSpec(memory_space=pltpu.VMEM)
    hbm = pl.BlockSpec(memory_space=pl.ANY)
    columns = jax.ShapeDtypeStruct((bunches, rows, BUNCH), F32)
    across_shape = jax.ShapeDtypeStruct((bunches, BUNCH, rows), F32)

    pieces, early, late, shifted, decay_out, decay_in, across, spread = pl.pallas_call(
        partial(states_kernel, heads, piece_rows),
        name="states",
        in_specs=[vmem] * 4 + [hbm] * 2,
        out_specs=[hbm] * 3 + [vmem] * 5,
        out_shape=[
            jax.ShapeDtypeStruct((count, 2 * piece_rows + 8, LANES), F32),
            jax.ShapeDtypeStruct((state, inner), F32),
            jax.ShapeDtypeStruct((state, inner), F32),
            columns,
            columns,
            columns,
            across_shape,
            jax.ShapeDtypeStruct((8, inner), F32),
        ],
        scratch_shapes=[
            pltpu.VMEM((rows, inner), BF16),
            pltpu.VMEM((rows, inner), BF16),
            pltpu.VMEM((count, 2 * piece_rows + 8, LANES), F32),
            pltpu.VMEM((state, inner), F32),
            pltpu.VMEM((state, inner), F32),
            pltpu.SemaphoreType.DMA((bunches, 2)),
            pltpu.SemaphoreType.DMA((bunches, 3)),
        ],
        compiler_params=pltpu.CompilerParams(vmem_limit_bytes=40 * MIB),
        cost_estimate=pl.CostEstimate(flops=4 * rows * state * inner, bytes_accessed=8 * MIB, transcendentals=0),
    )(step_size, scale, write_vectors, read_vectors, activation, upstream)

    got = lax.all_to_all(pieces, "seq", 0, 0)

    back, local_rows, write_part, read_part = pl.pallas_call(
        local_kernel,
        name="local",
        grid=(blocks, bunches),
        in_specs=[
            pl.BlockSpec((GROUP, wide), lambda b, g: (b, g)),
            pl.BlockSpec((GROUP, wide), lambda b, g: (b, g)),
            pl.BlockSpec((GROUP, state), lambda b, g: (b, 0)),
            pl.BlockSpec((GROUP, state), lambda b, g: (b, 0)),
            pl.BlockSpec((1, GROUP, BUNCH), lambda b, g: (g, b, 0)),
            pl.BlockSpec((1, BUNCH, GROUP), lambda b, g: (g, 0, b)),
        ],
        out_specs=[
            pl.BlockSpec((GROUP, wide), lambda b, g: (b, g)),
            pl.BlockSpec((1, BUNCH, GROUP), lambda b, g: (g, 0, b)),
            pl.BlockSpec((GROUP, state), lambda b, g: (b, 0)),
            pl.BlockSpec((GROUP, state), lambda b, g: (b, 0)),
        ],
        out_shape=[
            jax.ShapeDtypeStruct((rows, inner), F32),
            across_shape,
            jax.ShapeDtypeStruct((rows, state), F32),
            jax.ShapeDtypeStruct((rows, state), F32),
        ],
        scratch_shapes=[pltpu.VMEM((GROUP, GROUP), F32), pltpu.VMEM((GROUP, GROUP), F32)],
        compiler_params=pltpu.CompilerParams(vmem_limit_bytes=24 * MIB),
        cost_estimate=pl.CostEstimate(
            flops=20_000_000_000, bytes_accessed=8 * MIB, transcendentals=blocks * heads * GROUP * GROUP
        ),
    )(activation, upstream, write_vectors, read_vectors, shifted, across)

    carried = pl.pallas_call(
        partial(scan_kernel, piece_rows),
        name="scan",
        in_specs=[vmem],
        out_specs=vmem,
        out_shape=jax.ShapeDtypeStruct((count, 2 * piece_rows, LANES), F32),
        compiler_params=pltpu.CompilerParams(vmem_limit_bytes=16 * MIB),
    )(got)
    carried = lax.all_to_all(carried, "seq", 0, 0)

    few = BUNCH // 2 * (LANES // piece_rows)
    whole = pl.BlockSpec((rows, state), lambda g: (0, 0))
    return pl.pallas_call(
        partial(cross_kernel, heads, piece_rows),
        name="cross",
        grid=(bunches,),
        in_specs=[
            pl.BlockSpec((rows, wide), lambda g: (0, g)),
            pl.BlockSpec((rows, wide), lambda g: (0, g)),
            pl.BlockSpec((rows, wide), lambda g: (0, g)),
            pl.BlockSpec((few, 2 * piece_rows, LANES), lambda g: (g, 0, 0)),
            pl.BlockSpec((few, 2 * piece_rows + 8, LANES), lambda g: (g, 0, 0)),
            pl.BlockSpec((state, wide), lambda g: (0, g)),
            pl.BlockSpec((state, wide), lambda g: (0, g)),
            pl.BlockSpec((1, rows, BUNCH), lambda g: (g, 0, 0)),
            pl.BlockSpec((1, rows, BUNCH), lambda g: (g, 0, 0)),
            pl.BlockSpec((8, wide), lambda g: (0, g)),
            whole,
            whole,
            pl.BlockSpec((bunches, BUNCH, rows), lambda g: (0, 0, 0)),
            whole,
            whole,
            pl.BlockSpec((rows, heads), lambda g: (0, 0)),
            pl.BlockSpec((1, heads), lambda g: (0, 0)),
        ],
        out_specs=[
            pl.BlockSpec((rows, wide), lambda g: (0, g)),
            pl.BlockSpec((rows, heads), lambda g: (0, 0)),
            whole,
            whole,
        ],
        out_shape=[
            jax.ShapeDtypeStruct((rows, inner), BF16),
            jax.ShapeDtypeStruct((rows, heads), F32),
            jax.ShapeDtypeStruct((rows, state), F32),
            jax.ShapeDtypeStruct((rows, state), F32),
        ],
        scratch_shapes=[
            pltpu.VMEM((rows, LANES), F32),
            pltpu.VMEM((rows, LANES), F32),
            pltpu.VMEM((8, LANES), F32),
        ],
        compiler_params=pltpu.CompilerParams(vmem_limit_bytes=32 * MIB),
        cost_estimate=pl.CostEstimate(flops=8 * rows * state * inner, bytes_accessed=16 * MIB, transcendentals=0),
    )(
        activation, upstream, back, carried, pieces, early, late, decay_out, decay_in, spread,
        write_vectors, read_vectors, local_rows, write_part, read_part, step_size, scale,
    )


def solution(mesh):
    spread = P(("dp", "seq"), None)
    return jax.shard_map(
        on_device,
        mesh=mesh,
        in_specs=(spread, spread, P("dp"), spread, spread, spread),
        out_specs=(spread, spread, spread, spread),
        check_vma=False,
    )
```

```python
import math
from functools import partial

import jax
import jax.numpy as jnp
from jax import lax
from jax.experimental import pallas as pl
from jax.experimental.pallas import tpu as pltpu
from jax.sharding import PartitionSpec as P

GROUP = 256
LANES = 128
BUNCH = 8
LOG2E = math.log2(math.e)
F32 = jnp.float32
BF16 = jnp.bfloat16
MIB = 1 << 20
VMEM_LIMIT = 56 * MIB
AHEAD = 4


def dot_nn(a, b):
    return jnp.dot(a, b, preferred_element_type=F32)


def dot_nt(a, b):
    return lax.dot_general(a, b, (((1,), (1,)), ((), ())), preferred_element_type=F32)


def dot_tn(a, b):
    return lax.dot_general(a, b, (((0,), (0,)), ((), ())), preferred_element_type=F32)


def split(value, terms):
    parts = []
    for _ in range(terms):
        part = value.astype(BF16)
        parts.append(part)
        value = value - part.astype(F32)
    return jnp.concatenate(parts, axis=0)


def exact_dot(value, table):
    rows = value.shape[0]
    product = dot_nn(split(value, 3), table)
    return product[:rows] + product[rows : 2 * rows] + product[2 * rows :]


def left_half(rows):
    return lax.broadcasted_iota(jnp.int32, (rows, LANES), 1) < LANES // 2


def order_table(size, upper):
    row = lax.broadcasted_iota(jnp.int32, (size, size), 0)
    column = lax.broadcasted_iota(jnp.int32, (size, size), 1)
    return jnp.where(row <= column if upper else row >= column, 1.0, 0.0).astype(BF16)


def channel_table(heads, width):
    head = lax.broadcasted_iota(jnp.int32, (heads, width), 0)
    lane = lax.broadcasted_iota(jnp.int32, (heads, width), 1)
    return jnp.where(lane // (width // heads) == head, 1.0, 0.0)


def spread_heads(across, table):
    return dot_tn(split(across, 2), jnp.concatenate([table, table], axis=0))


def states_kernel(
    heads, piece_rows, dt_ref, scale_ref, write_ref, read_ref, act_ref, up_ref,
    pieces_ref, tables_ref, spread_hbm_ref, dt_buf, write_buf, read_buf, act_buf, up_buf, piece_buf, across_ref, spread_ref,
    in_sems, small_sems, out_sems,
):
    rows = dt_ref.shape[1]
    blocks = rows // GROUP
    bunches = heads // BUNCH
    wide = BUNCH // 2 * LANES
    small = [
        pltpu.make_async_copy(source, target, small_sems.at[which])
        for which, (source, target) in enumerate(
            ((dt_ref, dt_buf), (write_ref, write_buf), (read_ref, read_buf), (across_ref, tables_ref), (spread_ref, spread_hbm_ref))
        )
    ]
    loads = []
    for bunch in range(bunches):
        for which, (source, target) in enumerate(((act_ref, act_buf), (up_ref, up_buf))):
            lanes = pl.ds(bunch * wide, wide)
            loads.append(
                pltpu.make_async_copy(
                    source.at[:, lanes], target.at[:, lanes], in_sems.at[bunch, which]
                )
            )
    small[0].start()
    for copy in loads[:AHEAD]:
        copy.start()
    small[1].start()
    small[2].start()
    small[0].wait()
    same = lax.broadcasted_iota(jnp.int32, (heads, heads), 0) == lax.broadcasted_iota(
        jnp.int32, (heads, heads), 1
    )
    scale = jnp.sum(jnp.where(same, scale_ref[...], 0.0), axis=1, keepdims=True)
    dt = dt_buf[...]
    log_decay = dt * scale
    across_ref[4 * heads :, :] = log_decay
    order = order_table(GROUP, True)
    stacked = jnp.concatenate([log_decay[:, b * GROUP : (b + 1) * GROUP] for b in range(blocks)], axis=0)
    running = exact_dot(stacked, order)
    totals = running[:, GROUP - 1 : GROUP]
    entering = jnp.exp(running)
    leaving = jnp.exp(totals - running)
    for block in range(blocks):
        span = slice(block * GROUP, (block + 1) * GROUP)
        some = slice(block * heads, (block + 1) * heads)
        across_ref[:heads, span] = running[some] * LOG2E
        across_ref[heads : 2 * heads, span] = running[some] * LOG2E - jnp.log2(dt[:, span])
        across_ref[2 * heads : 3 * heads, span] = leaving[some] * dt[:, span]
        across_ref[3 * heads : 4 * heads, span] = entering[some]
    small[3].start()
    first_total, second_total = totals[:heads], totals[heads:]
    first_running, second_running = running[:heads], running[heads:] + first_total
    device_total = first_total + second_total
    device_in = jnp.concatenate([entering[:heads], jnp.exp(second_running)], axis=1)
    device_out = dt * jnp.concatenate(
        [jnp.exp(device_total - first_running), leaving[heads:]], axis=1
    )
    columns = [jnp.exp(first_total), jnp.exp(second_total), jnp.exp(device_total)]
    table = channel_table(BUNCH, wide)
    table_low = table.astype(BF16)
    for bunch in range(bunches):
        lanes = slice(bunch * wide, (bunch + 1) * wide)
        some = slice(bunch * BUNCH, (bunch + 1) * BUNCH)
        first, second, both = (
            jnp.sum(table * column[some], axis=0, keepdims=True) for column in columns
        )
        spread_ref[:, lanes] = jnp.concatenate([first, second, both, jnp.zeros((5, wide), F32)], axis=0)
    small[4].start()
    small[1].wait()
    write_across = write_buf[...].T
    small[2].wait()
    read_across = read_buf[...].T
    per_pair = LANES // piece_rows
    stores = []
    for bunch in range(bunches):
        lanes = slice(bunch * wide, (bunch + 1) * wide)
        some = slice(bunch * BUNCH, (bunch + 1) * BUNCH)
        both = spread_ref[2:3, lanes]
        loads[2 * bunch].wait()
        if 2 * bunch + AHEAD < len(loads):
            loads[2 * bunch + AHEAD].start()
        act_scaled = act_buf[:, lanes].astype(F32) * spread_heads(device_out[some], table_low)
        state = dot_nn(write_across, act_scaled.astype(BF16))
        loads[2 * bunch + 1].wait()
        if 2 * bunch + 1 + AHEAD < len(loads):
            loads[2 * bunch + 1 + AHEAD].start()
        up_scaled = up_buf[:, lanes].astype(F32) * spread_heads(device_in[some], table_low)
        grad = dot_nn(read_across, up_scaled.astype(BF16))
        for local in range(BUNCH // 2):
            pair = bunch * BUNCH // 2 + local
            here = slice(local * LANES, (local + 1) * LANES)
            few = slice(pair * per_pair, (pair + 1) * per_pair)
            piece_buf[few, :piece_rows, :] = state[:, here].reshape(per_pair, piece_rows, LANES)
            piece_buf[few, piece_rows : 2 * piece_rows, :] = grad[:, here].reshape(
                per_pair, piece_rows, LANES
            )
            piece_buf[few, 2 * piece_rows :, :] = jnp.broadcast_to(
                both[:, here][None], (per_pair, 8, LANES)
            )
        few = pl.ds(bunch * BUNCH // 2 * per_pair, BUNCH // 2 * per_pair)
        copy = pltpu.make_async_copy(piece_buf.at[few], pieces_ref.at[few], out_sems.at[bunch])
        copy.start()
        stores.append(copy)
    for copy in stores + small[3:]:
        copy.wait()


def scan_kernel(piece_rows, got_ref, after_ref, carried_ref):
    count = got_ref.shape[0]
    zero = jnp.zeros((piece_rows, LANES), F32)

    def lap(step, carry):
        state, grad = carry
        carried_ref[step, :piece_rows, :] = state
        state = got_ref[step, 2 * piece_rows : 2 * piece_rows + 1, :] * state + got_ref[step, :piece_rows, :]
        back = count - 1 - step
        carried_ref[back, piece_rows:, :] = grad
        grad = (
            got_ref[back, piece_rows : 2 * piece_rows, :]
            + got_ref[back, 2 * piece_rows : 2 * piece_rows + 1, :] * grad
        )
        return state, grad

    lax.fori_loop(0, count, lap, (zero, zero), unroll=8)


def local_kernel(
    act_ref, up_ref, write_ref, read_ref, running_ref, shifted_ref, out_ref, in_ref,
    back_ref, act_scaled_ref, up_scaled_ref, inside_ref, rows_ref, columns_ref, write_part_ref, read_part_ref, done_ref,
    pair_sum, scores,
):
    bunch = pl.program_id(1)
    half = GROUP // 2
    wide = act_ref.shape[1]
    triangle = lax.broadcasted_iota(jnp.int32, (half, half), 0) <= lax.broadcasted_iota(
        jnp.int32, (half, half), 1
    )

    @pl.when(bunch == 0)
    def _():
        scores[...] = dot_nt(write_ref[...], read_ref[...])
        pair_sum[...] = jnp.zeros_like(pair_sum)

    table = channel_table(BUNCH, wide).astype(BF16)
    act_scaled = (act_ref[...].astype(F32) * spread_heads(out_ref[...], table)).astype(BF16)
    up_scaled = (up_ref[...].astype(F32) * spread_heads(in_ref[...], table)).astype(BF16)
    act_scaled_ref[...] = act_scaled
    up_scaled_ref[...] = up_scaled

    @pl.when(pl.program_id(0) == 0)
    def _():
        inside_ref[0] = dot_tn(write_ref[...], act_scaled)

    @pl.when(pl.program_id(0) == 1)
    def _():
        inside_ref[0] = dot_tn(read_ref[...], up_scaled)

    shifted = jnp.concatenate([shifted_ref[...], jnp.zeros((LANES - BUNCH, GROUP), F32)], axis=0).T
    left = left_half(GROUP)
    lane = lax.broadcasted_iota(jnp.int32, (GROUP, LANES), 1)
    columns = jnp.zeros((GROUP, LANES), F32)
    for pair in range(BUNCH // 2):
        here = slice(pair * LANES, (pair + 1) * LANES)
        act = act_ref[:, here]
        up = up_ref[:, here]
        back_top = jnp.zeros((half, LANES), F32)
        back_low = jnp.zeros((half, LANES), F32)
        for side in range(2):
            head = 2 * pair + side
            keep = left if side == 0 else jnp.logical_not(left)
            act_one = jnp.where(keep, act, jnp.zeros_like(act))
            up_one = jnp.where(keep, up, jnp.zeros_like(up))
            late = running_ref[head : head + 1, :]
            soon = shifted[:, head : head + 1]
            decay_a = jnp.where(triangle, jnp.exp2(late[:, :half] - soon[:half]), 0.0)
            decay_b = jnp.exp2(late[:, half:] - soon[:half])
            decay_c = jnp.where(triangle, jnp.exp2(late[:, half:] - soon[half:]), 0.0)
            decay_top = jnp.concatenate([decay_a, decay_b], axis=1)
            dots_top = dot_nt(act_one[:half], up)
            dots_low = dot_nt(act_one[half:], up[half:])
            pair_sum[:half, :] += decay_top * dots_top
            pair_sum[half:, half:] += decay_c * dots_low
            masked_top = (decay_top * scores[:half, :]).astype(BF16)
            masked_low = (decay_c * scores[half:, half:]).astype(BF16)
            sums = jnp.sum(masked_top.astype(F32) * dots_top, axis=0, keepdims=True)
            low_sums = jnp.sum(masked_low.astype(F32) * dots_low, axis=0, keepdims=True)
            rows_ref[head : head + 1, :half] = sums[:, :half]
            rows_ref[head : head + 1, half:] = sums[:, half:] + low_sums
            back_top += dot_nn(masked_top, up_one)
            back_low += dot_nn(masked_low, up_one[half:])
        back = jnp.concatenate([back_top, back_low], axis=0)
        back_ref[:, here] = back.astype(BF16)
        product = act.astype(F32) * back
        for side in range(2):
            keep = left if side == 0 else jnp.logical_not(left)
            one = jnp.sum(jnp.where(keep, product, 0.0), axis=1, keepdims=True)
            columns = jnp.where(lane == 2 * pair + side, one, columns)
    columns_ref[...] = columns.T[:BUNCH]

    @pl.when(bunch == pl.num_programs(1) - 1)
    def _():
        low = pair_sum[...].astype(BF16)
        done_ref[...] = jnp.zeros_like(done_ref)
        write_part_ref[...] = dot_nn(low, read_ref[...])
        read_part_ref[...] = dot_tn(low, write_ref[...])


def halves(value):
    high = value.astype(BF16)
    return [high, (value - high.astype(F32)).astype(BF16)]


def cross_kernel(
    heads, piece_rows, act_scaled_ref, up_scaled_ref, back_ref, carried_ref, inside_ref, tables_ref, spread_ref,
    rows_ref, columns_ref, write_ref, read_ref, write_part_ref, read_part_ref,
    act_grad_ref, log_ref, write_grad_ref, read_grad_ref, act_grad_buf, sems,
):
    rows, inner = act_scaled_ref.shape
    blocks = rows // GROUP
    bunches = heads // BUNCH
    wide = inner // bunches
    per_pair = LANES // piece_rows

    def gather(low, bunch):
        return jnp.concatenate(
            [
                carried_ref[pair * per_pair : (pair + 1) * per_pair, low : low + piece_rows, :].reshape(
                    LANES, LANES
                )
                for pair in range(bunch * wide // LANES, (bunch + 1) * wide // LANES)
            ],
            axis=1,
        )

    table = channel_table(BUNCH, wide)
    table_low = table.astype(BF16)
    channel = lax.broadcasted_iota(jnp.int32, (2 * BUNCH, 4 * wide), 1)
    lane = lax.broadcasted_iota(jnp.int32, (2 * BUNCH, 4 * wide), 0)
    place = channel // (2 * wide) * BUNCH + channel % wide // (wide // BUNCH)
    gather_table = jnp.where(lane == place, 1.0, 0.0).astype(BF16)
    order = order_table(GROUP, False)
    copies = []
    for bunch in range(bunches):
        lanes = slice(bunch * wide, (bunch + 1) * wide)
        some = slice(bunch * BUNCH, (bunch + 1) * BUNCH)
        first, second = spread_ref[0:1, lanes], spread_ref[1:2, lanes]
        enter_0, leave_1 = gather(0, bunch), gather(piece_rows, bunch)
        kept_0, kept_1 = first * enter_0, second * leave_1
        enter_1 = kept_0 + inside_ref[0, :, lanes]
        leave_0 = inside_ref[1, :, lanes] + kept_1
        enters, leaves = (enter_0, enter_1), (leave_0, leave_1)
        edges = [
            jnp.sum(table * jnp.sum(product, axis=0, keepdims=True), axis=1, keepdims=True)
            for product in (leave_0 * kept_0, kept_1 * enter_1)
        ]
        nets, cols = [], []
        for block in range(blocks):
            span = slice(block * GROUP, (block + 1) * GROUP)
            enter_low = enters[block].astype(BF16)
            leave_low = leaves[block].astype(BF16)
            offset = dot_nn(read_ref[span, :], enter_low)
            cross = dot_nn(write_ref[span, :], leave_low)
            decay_out = spread_heads(tables_ref[2 * heads + bunch * BUNCH : 2 * heads + (bunch + 1) * BUNCH, span], table_low)
            act_grad_buf[span, lanes] = (back_ref[span, lanes].astype(F32) + decay_out * cross).astype(BF16)
            act_scaled, up_scaled = act_scaled_ref[span, lanes], up_scaled_ref[span, lanes]
            row_products = offset * up_scaled.astype(F32)
            col_products = cross * act_scaled.astype(F32)
            sums = dot_nt(
                gather_table, jnp.concatenate(halves(row_products) + halves(col_products), axis=1)
            )
            column = columns_ref[some, span] + sums[BUNCH:]
            nets.append(rows_ref[some, span] + sums[:BUNCH] - column)
            cols.append(column)
            edges[block] += jnp.sum(sums[BUNCH:], axis=1, keepdims=True)
            read_cross = dot_nt(up_scaled, enter_low)
            write_cross = dot_nt(act_scaled, leave_low)
            if bunch == 0:
                read_grad_ref[span, :] = read_part_ref[span, :] + read_cross
                write_grad_ref[span, :] = write_part_ref[span, :] + write_cross
            else:
                read_grad_ref[span, :] += read_cross
                write_grad_ref[span, :] += write_cross
        few = pl.ds(bunch * wide, wide)
        copy = pltpu.make_async_copy(act_grad_buf.at[:, few], act_grad_ref.at[:, few], sems.at[bunch])
        copy.start()
        copies.append(copy)
        suffix = exact_dot(jnp.concatenate(nets, axis=0), order)
        for block in range(blocks):
            span = slice(block * GROUP, (block + 1) * GROUP)
            log_grad = suffix[block * BUNCH : (block + 1) * BUNCH] + edges[block]
            log_ref[some, span] = cols[block] + tables_ref[4 * heads + bunch * BUNCH : 4 * heads + (bunch + 1) * BUNCH, span] * log_grad
    for copy in copies:
        copy.wait()


def on_device(activation, step_size, decay_scale, write_vectors, read_vectors, upstream):
    rows, inner = activation.shape
    heads = decay_scale.shape[0]
    state = write_vectors.shape[1]
    count = lax.axis_size("seq")
    pairs = heads // 2
    piece_rows = pairs * state // count
    bunches = heads // BUNCH
    blocks = rows // GROUP
    wide = inner // bunches
    scale = decay_scale.reshape(1, heads)
    vmem = pl.BlockSpec(memory_space=pltpu.VMEM)
    hbm = pl.BlockSpec(memory_space=pl.ANY)
    across = jax.ShapeDtypeStruct((heads, rows), F32)
    low = jax.ShapeDtypeStruct((rows, inner), BF16)
    part = jax.ShapeDtypeStruct((rows, state), F32)

    pieces, tables, spread = pl.pallas_call(
        partial(states_kernel, heads, piece_rows),
        name="states",
        in_specs=[hbm, vmem] + [hbm] * 4,
        out_specs=[hbm] * 3,
        out_shape=[
            jax.ShapeDtypeStruct((count, 2 * piece_rows + 8, LANES), F32),
            jax.ShapeDtypeStruct((5 * heads, rows), F32),
            jax.ShapeDtypeStruct((8, inner), F32),
        ],
        scratch_shapes=[
            pltpu.VMEM((heads, rows), F32),
            pltpu.VMEM((rows, state), BF16),
            pltpu.VMEM((rows, state), BF16),
            pltpu.VMEM((rows, inner), BF16),
            pltpu.VMEM((rows, inner), BF16),
            pltpu.VMEM((count, 2 * piece_rows + 8, LANES), F32),
            pltpu.VMEM((5 * heads, rows), F32),
            pltpu.VMEM((8, inner), F32),
            pltpu.SemaphoreType.DMA((bunches, 2)),
            pltpu.SemaphoreType.DMA((5,)),
            pltpu.SemaphoreType.DMA((bunches,)),
        ],
        compiler_params=pltpu.CompilerParams(vmem_limit_bytes=VMEM_LIMIT),
        cost_estimate=pl.CostEstimate(flops=4 * rows * state * inner, bytes_accessed=8 * MIB, transcendentals=0),
    )(step_size.T, scale, write_vectors, read_vectors, activation, upstream)

    got = lax.all_to_all(pieces, "seq", 0, 0)

    narrow = pl.BlockSpec((BUNCH, GROUP), lambda b, g: (g, b))
    def table(which):
        return pl.BlockSpec((BUNCH, GROUP), lambda b, g: (which * bunches + g, b))

    block_wide = pl.BlockSpec((GROUP, wide), lambda b, g: (b, g))
    block_state = pl.BlockSpec((GROUP, state), lambda b, g: (b, 0))
    back, act_scaled, up_scaled, inside, local_rows, local_columns, write_part, read_part, done = pl.pallas_call(
        local_kernel,
        name="local",
        grid=(blocks, bunches),
        in_specs=[block_wide, block_wide, block_state, block_state] + [table(i) for i in range(4)],
        out_specs=[
            block_wide,
            block_wide,
            block_wide,
            pl.BlockSpec((1, state, wide), lambda b, g: (b, 0, g)),
            narrow,
            narrow,
            block_state,
            block_state,
            pl.BlockSpec((8, LANES), lambda b, g: (0, 0)),
        ],
        out_shape=[low, low, low, jax.ShapeDtypeStruct((blocks, state, inner), F32), across, across, part, part, jax.ShapeDtypeStruct((8, LANES), F32)],
        scratch_shapes=[pltpu.VMEM((GROUP, GROUP), F32), pltpu.VMEM((GROUP, GROUP), F32)],
        compiler_params=pltpu.CompilerParams(vmem_limit_bytes=16 * MIB),
        cost_estimate=pl.CostEstimate(
            flops=20_000_000_000, bytes_accessed=8 * MIB, transcendentals=blocks * heads * GROUP * GROUP
        ),
    )(activation, upstream, write_vectors, read_vectors, tables, tables, tables, tables)

    carried = pl.pallas_call(
        partial(scan_kernel, piece_rows),
        name="scan",
        in_specs=[vmem, pl.BlockSpec(memory_space=pltpu.HBM)],
        out_specs=vmem,
        out_shape=jax.ShapeDtypeStruct((count, 2 * piece_rows, LANES), F32),
        compiler_params=pltpu.CompilerParams(vmem_limit_bytes=8 * MIB),
    )(got, done)
    carried = lax.all_to_all(carried, "seq", 0, 0)

    act_grad, log_grad, write_grad, read_grad = pl.pallas_call(
        partial(cross_kernel, heads, piece_rows),
        name="cross",
        in_specs=[vmem] * 13,
        out_specs=[hbm] + [vmem] * 3,
        out_shape=[low, across, part, part],
        scratch_shapes=[pltpu.VMEM((rows, inner), BF16), pltpu.SemaphoreType.DMA((bunches,))],
        compiler_params=pltpu.CompilerParams(vmem_limit_bytes=16 * MIB),
        cost_estimate=pl.CostEstimate(flops=8 * rows * state * inner, bytes_accessed=16 * MIB, transcendentals=0),
    )(
        act_scaled, up_scaled, back, carried, inside, tables, spread, local_rows, local_columns,
        write_vectors, read_vectors, write_part, read_part,
    )
    return act_grad, log_grad.T, write_grad, read_grad


def solution(mesh):
    spread = P(("dp", "seq"), None)
    return jax.shard_map(
        on_device,
        mesh=mesh,
        in_specs=(spread, spread, P("dp"), spread, spread, spread),
        out_specs=(spread, spread, spread, spread),
        check_vma=False,
    )
```

```python
import math
from functools import partial

import jax
import jax.numpy as jnp
from jax import lax
from jax.experimental import pallas as pl
from jax.experimental.pallas import tpu as pltpu
from jax.sharding import PartitionSpec as P

GROUP = 256
LANES = 128
BUNCH = 8
LOG2E = math.log2(math.e)
F32 = jnp.float32
BF16 = jnp.bfloat16
MIB = 1 << 20
VMEM_LIMIT = 56 * MIB
AHEAD = 4


def dot_nn(a, b):
    return jnp.dot(a, b, preferred_element_type=F32)


def dot_nt(a, b):
    return lax.dot_general(a, b, (((1,), (1,)), ((), ())), preferred_element_type=F32)


def dot_tn(a, b):
    return lax.dot_general(a, b, (((0,), (0,)), ((), ())), preferred_element_type=F32)


def split(value, terms):
    parts = []
    for _ in range(terms):
        part = value.astype(BF16)
        parts.append(part)
        value = value - part.astype(F32)
    return jnp.concatenate(parts, axis=0)


def exact_dot(value, table):
    rows = value.shape[0]
    product = dot_nn(split(value, 3), table)
    return product[:rows] + product[rows : 2 * rows] + product[2 * rows :]


def left_half(rows):
    return lax.broadcasted_iota(jnp.int32, (rows, LANES), 1) < LANES // 2


def order_table(size, upper):
    row = lax.broadcasted_iota(jnp.int32, (size, size), 0)
    column = lax.broadcasted_iota(jnp.int32, (size, size), 1)
    return jnp.where(row <= column if upper else row >= column, 1.0, 0.0).astype(BF16)


def channel_table(heads, width):
    head = lax.broadcasted_iota(jnp.int32, (heads, width), 0)
    lane = lax.broadcasted_iota(jnp.int32, (heads, width), 1)
    return jnp.where(lane // (width // heads) == head, 1.0, 0.0)


def spread_heads(across, table):
    return dot_tn(split(across, 2), jnp.concatenate([table, table], axis=0))


def states_kernel(
    heads, piece_rows, dt_ref, scale_ref, write_ref, read_ref, act_ref, up_ref,
    pieces_ref, tables_ref, spread_hbm_ref, dt_buf, write_buf, read_buf, act_buf, up_buf, piece_buf, across_ref, spread_ref,
    in_sems, small_sems, out_sems,
):
    rows = dt_ref.shape[1]
    blocks = rows // GROUP
    bunches = heads // BUNCH
    wide = BUNCH // 2 * LANES
    small = [
        pltpu.make_async_copy(source, target, small_sems.at[which])
        for which, (source, target) in enumerate(
            ((dt_ref, dt_buf), (write_ref, write_buf), (read_ref, read_buf), (across_ref, tables_ref), (spread_ref, spread_hbm_ref))
        )
    ]
    loads = []
    for bunch in range(bunches):
        for which, (source, target) in enumerate(((act_ref, act_buf), (up_ref, up_buf))):
            lanes = pl.ds(bunch * wide, wide)
            loads.append(
                pltpu.make_async_copy(
                    source.at[:, lanes], target.at[:, lanes], in_sems.at[bunch, which]
                )
            )
    small[0].start()
    for copy in loads[:AHEAD]:
        copy.start()
    small[1].start()
    small[2].start()
    small[0].wait()
    same = lax.broadcasted_iota(jnp.int32, (heads, heads), 0) == lax.broadcasted_iota(
        jnp.int32, (heads, heads), 1
    )
    scale = jnp.sum(jnp.where(same, scale_ref[...], 0.0), axis=1, keepdims=True)
    dt = dt_buf[...]
    log_decay = dt * scale
    across_ref[4 * heads :, :] = log_decay
    order = order_table(GROUP, True)
    stacked = jnp.concatenate([log_decay[:, b * GROUP : (b + 1) * GROUP] for b in range(blocks)], axis=0)
    running = exact_dot(stacked, order)
    totals = running[:, GROUP - 1 : GROUP]
    entering = jnp.exp(running)
    leaving = jnp.exp(totals - running)
    for block in range(blocks):
        span = slice(block * GROUP, (block + 1) * GROUP)
        some = slice(block * heads, (block + 1) * heads)
        across_ref[:heads, span] = running[some] * LOG2E
        across_ref[heads : 2 * heads, span] = running[some] * LOG2E - jnp.log2(dt[:, span])
        across_ref[2 * heads : 3 * heads, span] = leaving[some] * dt[:, span]
        across_ref[3 * heads : 4 * heads, span] = entering[some]
    small[3].start()
    first_total, second_total = totals[:heads], totals[heads:]
    first_running, second_running = running[:heads], running[heads:] + first_total
    device_total = first_total + second_total
    device_in = jnp.concatenate([entering[:heads], jnp.exp(second_running)], axis=1)
    device_out = dt * jnp.concatenate(
        [jnp.exp(device_total - first_running), leaving[heads:]], axis=1
    )
    columns = [jnp.exp(first_total), jnp.exp(second_total), jnp.exp(device_total)]
    table = channel_table(BUNCH, wide)
    table_low = table.astype(BF16)
    for bunch in range(bunches):
        lanes = slice(bunch * wide, (bunch + 1) * wide)
        some = slice(bunch * BUNCH, (bunch + 1) * BUNCH)
        first, second, both = (
            jnp.sum(table * column[some], axis=0, keepdims=True) for column in columns
        )
        spread_ref[:, lanes] = jnp.concatenate([first, second, both, jnp.zeros((5, wide), F32)], axis=0)
    small[4].start()
    small[1].wait()
    write_across = write_buf[...].T
    small[2].wait()
    read_across = read_buf[...].T
    per_pair = LANES // piece_rows
    stores = []
    for bunch in range(bunches):
        lanes = slice(bunch * wide, (bunch + 1) * wide)
        some = slice(bunch * BUNCH, (bunch + 1) * BUNCH)
        both = spread_ref[2:3, lanes]
        loads[2 * bunch].wait()
        if 2 * bunch + AHEAD < len(loads):
            loads[2 * bunch + AHEAD].start()
        act_scaled = act_buf[:, lanes].astype(F32) * spread_heads(device_out[some], table_low)
        state = dot_nn(write_across, act_scaled.astype(BF16))
        loads[2 * bunch + 1].wait()
        if 2 * bunch + 1 + AHEAD < len(loads):
            loads[2 * bunch + 1 + AHEAD].start()
        up_scaled = up_buf[:, lanes].astype(F32) * spread_heads(device_in[some], table_low)
        grad = dot_nn(read_across, up_scaled.astype(BF16))
        for local in range(BUNCH // 2):
            pair = bunch * BUNCH // 2 + local
            here = slice(local * LANES, (local + 1) * LANES)
            few = slice(pair * per_pair, (pair + 1) * per_pair)
            piece_buf[few, :piece_rows, :] = state[:, here].reshape(per_pair, piece_rows, LANES)
            piece_buf[few, piece_rows : 2 * piece_rows, :] = grad[:, here].reshape(
                per_pair, piece_rows, LANES
            )
            piece_buf[few, 2 * piece_rows :, :] = jnp.broadcast_to(
                both[:, here][None], (per_pair, 8, LANES)
            )
        few = pl.ds(bunch * BUNCH // 2 * per_pair, BUNCH // 2 * per_pair)
        copy = pltpu.make_async_copy(piece_buf.at[few], pieces_ref.at[few], out_sems.at[bunch])
        copy.start()
        stores.append(copy)
    for copy in stores + small[3:]:
        copy.wait()


def scan_kernel(piece_rows, got_ref, after_ref, carried_ref):
    count = got_ref.shape[0]
    zero = jnp.zeros((piece_rows, LANES), F32)

    def lap(step, carry):
        state, grad = carry
        carried_ref[step, :piece_rows, :] = state
        state = got_ref[step, 2 * piece_rows : 2 * piece_rows + 1, :] * state + got_ref[step, :piece_rows, :]
        back = count - 1 - step
        carried_ref[back, piece_rows:, :] = grad
        grad = (
            got_ref[back, piece_rows : 2 * piece_rows, :]
            + got_ref[back, 2 * piece_rows : 2 * piece_rows + 1, :] * grad
        )
        return state, grad

    lax.fori_loop(0, count, lap, (zero, zero), unroll=8)


def local_kernel(
    act_ref, up_ref, write_ref, read_ref, running_ref, shifted_ref, out_ref, in_ref,
    back_ref, act_scaled_ref, up_scaled_ref, inside_ref, write_part_ref, read_part_ref, done_ref,
    pair_sum, scores,
):
    bunch = pl.program_id(1)
    half = GROUP // 2
    wide = act_ref.shape[1]
    state = write_ref.shape[1]
    triangle = lax.broadcasted_iota(jnp.int32, (half, half), 0) <= lax.broadcasted_iota(
        jnp.int32, (half, half), 1
    )

    @pl.when(bunch == 0)
    def _():
        scores[...] = dot_nt(write_ref[...], read_ref[...])
        pair_sum[...] = jnp.zeros_like(pair_sum)

    table = channel_table(BUNCH, wide).astype(BF16)
    act_scaled = (act_ref[...].astype(F32) * spread_heads(out_ref[...], table)).astype(BF16)
    up_scaled = (up_ref[...].astype(F32) * spread_heads(in_ref[...], table)).astype(BF16)
    act_scaled_ref[...] = act_scaled.T
    up_scaled_ref[...] = up_scaled.T

    @pl.when(pl.program_id(0) == 0)
    def _():
        inside_ref[0, :state, :] = dot_tn(write_ref[...], act_scaled)

    @pl.when(pl.program_id(0) == 1)
    def _():
        inside_ref[0, :state, :] = dot_tn(read_ref[...], up_scaled)

    shifted = jnp.concatenate([shifted_ref[...], jnp.zeros((LANES - BUNCH, GROUP), F32)], axis=0).T
    left = left_half(GROUP)
    lane = lax.broadcasted_iota(jnp.int32, (GROUP, LANES), 1)
    columns = jnp.zeros((GROUP, LANES), F32)
    for pair in range(BUNCH // 2):
        here = slice(pair * LANES, (pair + 1) * LANES)
        act = act_ref[:, here]
        up = up_ref[:, here]
        back_top = jnp.zeros((half, LANES), F32)
        back_low = jnp.zeros((half, LANES), F32)
        for side in range(2):
            head = 2 * pair + side
            keep = left if side == 0 else jnp.logical_not(left)
            act_one = jnp.where(keep, act, jnp.zeros_like(act))
            up_one = jnp.where(keep, up, jnp.zeros_like(up))
            late = running_ref[head : head + 1, :]
            soon = shifted[:, head : head + 1]
            decay_a = jnp.where(triangle, jnp.exp2(late[:, :half] - soon[:half]), 0.0)
            decay_b = jnp.exp2(late[:, half:] - soon[:half])
            decay_c = jnp.where(triangle, jnp.exp2(late[:, half:] - soon[half:]), 0.0)
            decay_top = jnp.concatenate([decay_a, decay_b], axis=1)
            dots_top = dot_nt(act_one[:half], up)
            dots_low = dot_nt(act_one[half:], up[half:])
            pair_sum[:half, :] += decay_top * dots_top
            pair_sum[half:, half:] += decay_c * dots_low
            masked_top = (decay_top * scores[:half, :]).astype(BF16)
            masked_low = (decay_c * scores[half:, half:]).astype(BF16)
            sums = jnp.sum(masked_top.astype(F32) * dots_top, axis=0, keepdims=True)
            low_sums = jnp.sum(masked_low.astype(F32) * dots_low, axis=0, keepdims=True)
            inside_ref[0, state + head : state + head + 1, :half] = sums[:, :half]
            inside_ref[0, state + head : state + head + 1, half:GROUP] = sums[:, half:] + low_sums
            back_top += dot_nn(masked_top, up_one)
            back_low += dot_nn(masked_low, up_one[half:])
        back = jnp.concatenate([back_top, back_low], axis=0)
        back_ref[:, here] = back.astype(BF16)
        product = act.astype(F32) * back
        for side in range(2):
            keep = left if side == 0 else jnp.logical_not(left)
            one = jnp.sum(jnp.where(keep, product, 0.0), axis=1, keepdims=True)
            columns = jnp.where(lane == 2 * pair + side, one, columns)
    inside_ref[0, state + BUNCH :, :GROUP] = columns.T[:BUNCH]

    @pl.when(bunch == pl.num_programs(1) - 1)
    def _():
        low = pair_sum[...].astype(BF16)
        done_ref[...] = jnp.zeros_like(done_ref)
        write_part_ref[...] = dot_nn(low, read_ref[...])
        read_part_ref[...] = dot_tn(low, write_ref[...])


def cross_kernel(
    heads, piece_rows, act_scaled_ref, up_scaled_ref, back_ref, carried_ref, inside_ref, tables_ref, spread_ref,
    write_ref, read_ref, write_part_ref, read_part_ref,
    act_grad_ref, log_ref, write_grad_ref, read_grad_ref, act_grad_buf, read_acc, write_acc, read_buf, write_buf, sems, part_sems,
):
    inner, rows = act_scaled_ref.shape
    blocks = rows // GROUP
    bunches = heads // BUNCH
    channels = inner // heads
    state = write_ref.shape[1]
    parts = [
        pltpu.make_async_copy(source, target, part_sems.at[which])
        for which, (source, target) in enumerate(((write_part_ref, write_buf), (read_part_ref, read_buf)))
    ]
    for copy in parts:
        copy.start()
    wide = inner // bunches
    per_pair = LANES // piece_rows

    def gather(low, bunch):
        return jnp.concatenate(
            [
                carried_ref[pair * per_pair : (pair + 1) * per_pair, low : low + piece_rows, :].reshape(
                    LANES, LANES
                )
                for pair in range(bunch * wide // LANES, (bunch + 1) * wide // LANES)
            ],
            axis=1,
        )

    table = channel_table(BUNCH, wide)
    table_low = table.astype(BF16)
    write_across = [write_ref[b * GROUP : (b + 1) * GROUP, :].T for b in range(blocks)]
    read_across = [read_ref[b * GROUP : (b + 1) * GROUP, :].T for b in range(blocks)]

    def head_sums(product):
        return jnp.concatenate(
            [
                jnp.sum(product[h * channels : (h + 1) * channels], axis=0, keepdims=True)
                for h in range(BUNCH)
            ],
            axis=0,
        )

    order = order_table(GROUP, False)
    copies = []
    for bunch in range(bunches):
        if bunch == bunches - 1:
            for copy in parts:
                copy.wait()
        lanes = slice(bunch * wide, (bunch + 1) * wide)
        some = slice(bunch * BUNCH, (bunch + 1) * BUNCH)
        first, second = spread_ref[0:1, lanes], spread_ref[1:2, lanes]
        enter_0, leave_1 = gather(0, bunch), gather(piece_rows, bunch)
        kept_0, kept_1 = first * enter_0, second * leave_1
        enter_1 = kept_0 + inside_ref[0, :state, lanes]
        leave_0 = inside_ref[1, :state, lanes] + kept_1
        enters, leaves = (enter_0, enter_1), (leave_0, leave_1)
        edges = [
            jnp.sum(table * jnp.sum(product, axis=0, keepdims=True), axis=1, keepdims=True)
            for product in (leave_0 * kept_0, kept_1 * enter_1)
        ]
        nets, cols = [], []
        for block in range(blocks):
            span = slice(block * GROUP, (block + 1) * GROUP)
            enter_low = enters[block].astype(BF16)
            leave_low = leaves[block].astype(BF16)
            cross = dot_nn(write_ref[span, :], leave_low)
            decay_out = spread_heads(tables_ref[2 * heads + bunch * BUNCH : 2 * heads + (bunch + 1) * BUNCH, span], table_low)
            act_grad_buf[span, lanes] = (back_ref[span, lanes].astype(F32) + decay_out * cross).astype(BF16)
            act_scaled, up_scaled = act_scaled_ref[lanes, span], up_scaled_ref[lanes, span]
            row_sums = head_sums(dot_tn(enter_low, read_across[block]) * up_scaled.astype(F32))
            col_sums = head_sums(dot_tn(leave_low, write_across[block]) * act_scaled.astype(F32))
            near = slice(bunch * wide, bunch * wide + GROUP)
            column = inside_ref[block, state + BUNCH :, near] + col_sums
            nets.append(inside_ref[block, state : state + BUNCH, near] + row_sums - column)
            cols.append(column)
            edges[block] += jnp.sum(col_sums, axis=1, keepdims=True)
            read_cross = dot_nn(enter_low, up_scaled)
            write_cross = dot_nn(leave_low, act_scaled)
            if bunch == 0:
                read_acc[:, span] = read_cross
                write_acc[:, span] = write_cross
            elif bunch < bunches - 1:
                read_acc[:, span] += read_cross
                write_acc[:, span] += write_cross
            else:
                read_buf[span, :] += (read_acc[:, span] + read_cross).T
                write_buf[span, :] += (write_acc[:, span] + write_cross).T
        few = pl.ds(bunch * wide, wide)
        copy = pltpu.make_async_copy(act_grad_buf.at[:, few], act_grad_ref.at[:, few], sems.at[bunch])
        copy.start()
        copies.append(copy)
        suffix = exact_dot(jnp.concatenate(nets, axis=0), order)
        for block in range(blocks):
            span = slice(block * GROUP, (block + 1) * GROUP)
            log_grad = suffix[block * BUNCH : (block + 1) * BUNCH] + edges[block]
            log_ref[some, span] = cols[block] + tables_ref[4 * heads + bunch * BUNCH : 4 * heads + (bunch + 1) * BUNCH, span] * log_grad
    for which, (source, target) in enumerate(((write_buf, write_grad_ref), (read_buf, read_grad_ref))):
        copy = pltpu.make_async_copy(source, target, part_sems.at[2 + which])
        copy.start()
        copies.append(copy)
    for copy in copies:
        copy.wait()


def on_device(activation, step_size, decay_scale, write_vectors, read_vectors, upstream):
    rows, inner = activation.shape
    heads = decay_scale.shape[0]
    state = write_vectors.shape[1]
    count = lax.axis_size("seq")
    pairs = heads // 2
    piece_rows = pairs * state // count
    bunches = heads // BUNCH
    blocks = rows // GROUP
    wide = inner // bunches
    scale = decay_scale.reshape(1, heads)
    vmem = pl.BlockSpec(memory_space=pltpu.VMEM)
    hbm = pl.BlockSpec(memory_space=pl.ANY)
    across = jax.ShapeDtypeStruct((heads, rows), F32)
    low = jax.ShapeDtypeStruct((rows, inner), BF16)
    low_across = jax.ShapeDtypeStruct((inner, rows), BF16)
    part = jax.ShapeDtypeStruct((rows, state), F32)

    pieces, tables, spread = pl.pallas_call(
        partial(states_kernel, heads, piece_rows),
        name="states",
        in_specs=[hbm, vmem] + [hbm] * 4,
        out_specs=[hbm] * 3,
        out_shape=[
            jax.ShapeDtypeStruct((count, 2 * piece_rows + 8, LANES), F32),
            jax.ShapeDtypeStruct((5 * heads, rows), F32),
            jax.ShapeDtypeStruct((8, inner), F32),
        ],
        scratch_shapes=[
            pltpu.VMEM((heads, rows), F32),
            pltpu.VMEM((rows, state), BF16),
            pltpu.VMEM((rows, state), BF16),
            pltpu.VMEM((rows, inner), BF16),
            pltpu.VMEM((rows, inner), BF16),
            pltpu.VMEM((count, 2 * piece_rows + 8, LANES), F32),
            pltpu.VMEM((5 * heads, rows), F32),
            pltpu.VMEM((8, inner), F32),
            pltpu.SemaphoreType.DMA((bunches, 2)),
            pltpu.SemaphoreType.DMA((5,)),
            pltpu.SemaphoreType.DMA((bunches,)),
        ],
        compiler_params=pltpu.CompilerParams(vmem_limit_bytes=VMEM_LIMIT),
        cost_estimate=pl.CostEstimate(flops=4 * rows * state * inner, bytes_accessed=8 * MIB, transcendentals=0),
    )(step_size.T, scale, write_vectors, read_vectors, activation, upstream)

    got = lax.all_to_all(pieces, "seq", 0, 0)

    def table(which):
        return pl.BlockSpec((BUNCH, GROUP), lambda b, g: (which * bunches + g, b))

    block_wide = pl.BlockSpec((GROUP, wide), lambda b, g: (b, g))
    block_tall = pl.BlockSpec((wide, GROUP), lambda b, g: (g, b))
    block_state = pl.BlockSpec((GROUP, state), lambda b, g: (b, 0))
    back, act_scaled, up_scaled, inside, write_part, read_part, done = pl.pallas_call(
        local_kernel,
        name="local",
        grid=(blocks, bunches),
        in_specs=[block_wide, block_wide, block_state, block_state] + [table(i) for i in range(4)],
        out_specs=[
            block_wide,
            block_tall,
            block_tall,
            pl.BlockSpec((1, state + 2 * BUNCH, wide), lambda b, g: (b, 0, g)),
            block_state,
            block_state,
            pl.BlockSpec((8, LANES), lambda b, g: (0, 0)),
        ],
        out_shape=[low, low_across, low_across, jax.ShapeDtypeStruct((blocks, state + 2 * BUNCH, inner), F32), part, part, jax.ShapeDtypeStruct((8, LANES), F32)],
        scratch_shapes=[pltpu.VMEM((GROUP, GROUP), F32), pltpu.VMEM((GROUP, GROUP), F32)],
        compiler_params=pltpu.CompilerParams(vmem_limit_bytes=56 * MIB),
        cost_estimate=pl.CostEstimate(
            flops=20_000_000_000, bytes_accessed=8 * MIB, transcendentals=blocks * heads * GROUP * GROUP
        ),
    )(activation, upstream, write_vectors, read_vectors, tables, tables, tables, tables)

    carried = pl.pallas_call(
        partial(scan_kernel, piece_rows),
        name="scan",
        in_specs=[vmem, pl.BlockSpec(memory_space=pltpu.HBM)],
        out_specs=vmem,
        out_shape=jax.ShapeDtypeStruct((count, 2 * piece_rows, LANES), F32),
        compiler_params=pltpu.CompilerParams(vmem_limit_bytes=8 * MIB),
    )(got, done)
    carried = lax.all_to_all(carried, "seq", 0, 0)

    act_grad, log_grad, write_grad, read_grad = pl.pallas_call(
        partial(cross_kernel, heads, piece_rows),
        name="cross",
        in_specs=[vmem] * 9 + [hbm] * 2,
        out_specs=[hbm, vmem, hbm, hbm],
        input_output_aliases={9: 2, 10: 3},
        out_shape=[low, across, part, part],
        scratch_shapes=[
            pltpu.VMEM((rows, inner), BF16),
            pltpu.VMEM((state, rows), F32),
            pltpu.VMEM((state, rows), F32),
            pltpu.VMEM((rows, state), F32),
            pltpu.VMEM((rows, state), F32),
            pltpu.SemaphoreType.DMA((bunches,)),
            pltpu.SemaphoreType.DMA((4,)),
        ],
        compiler_params=pltpu.CompilerParams(vmem_limit_bytes=16 * MIB),
        cost_estimate=pl.CostEstimate(flops=8 * rows * state * inner, bytes_accessed=16 * MIB, transcendentals=0),
    )(
        act_scaled, up_scaled, back, carried, inside, tables, spread,
        write_vectors, read_vectors, write_part, read_part,
    )
    return act_grad, log_grad.T, write_grad, read_grad


def solution(mesh):
    spread = P(("dp", "seq"), None)
    return jax.shard_map(
        on_device,
        mesh=mesh,
        in_specs=(spread, spread, P("dp"), spread, spread, spread),
        out_specs=(spread, spread, spread, spread),
        check_vma=False,
    )
```

```python
import math
from functools import partial

import jax
import jax.numpy as jnp
from jax import lax
from jax.experimental import pallas as pl
from jax.experimental.pallas import tpu as pltpu
from jax.sharding import PartitionSpec as P

GROUP = 256
LANES = 128
BUNCH = 8
LOG2E = math.log2(math.e)
F32 = jnp.float32
BF16 = jnp.bfloat16
MIB = 1 << 20
VMEM_LIMIT = 56 * MIB
AHEAD = 2
STEP = 16


def dot_nn(a, b):
    return jnp.dot(a, b, preferred_element_type=F32)


def dot_nt(a, b):
    return lax.dot_general(a, b, (((1,), (1,)), ((), ())), preferred_element_type=F32)


def dot_tn(a, b):
    return lax.dot_general(a, b, (((0,), (0,)), ((), ())), preferred_element_type=F32)


def split(value, terms):
    parts = []
    for _ in range(terms):
        part = value.astype(BF16)
        parts.append(part)
        value = value - part.astype(F32)
    return jnp.concatenate(parts, axis=0)


def exact_dot(value, table):
    rows = value.shape[0]
    product = dot_nn(split(value, 3), table)
    return product[:rows] + product[rows : 2 * rows] + product[2 * rows :]


def left_half(rows):
    return lax.broadcasted_iota(jnp.int32, (rows, LANES), 1) < LANES // 2


def order_table(size, upper):
    row = lax.broadcasted_iota(jnp.int32, (size, size), 0)
    column = lax.broadcasted_iota(jnp.int32, (size, size), 1)
    return jnp.where(row <= column if upper else row >= column, 1.0, 0.0).astype(BF16)


def channel_table(heads, width):
    head = lax.broadcasted_iota(jnp.int32, (heads, width), 0)
    lane = lax.broadcasted_iota(jnp.int32, (heads, width), 1)
    return jnp.where(lane // (width // heads) == head, 1.0, 0.0)


def spread_heads(across, table):
    return dot_tn(split(across, 2), jnp.concatenate([table, table], axis=0))


def states_kernel(
    heads, piece_rows, dt_ref, scale_ref, write_ref, read_ref, act_ref, up_ref,
    pieces_ref, tables_ref, spread_hbm_ref, dt_buf, write_buf, read_buf, act_buf, up_buf, piece_buf, across_ref, spread_ref,
    in_sems, small_sems, out_sems,
):
    rows = dt_ref.shape[1]
    blocks = rows // GROUP
    bunches = heads // STEP
    wide = STEP // 2 * LANES
    small = [
        pltpu.make_async_copy(source, target, small_sems.at[which])
        for which, (source, target) in enumerate(
            ((dt_ref, dt_buf), (write_ref, write_buf), (read_ref, read_buf), (across_ref, tables_ref), (spread_ref, spread_hbm_ref))
        )
    ]
    loads = []
    for bunch in range(bunches):
        for which, (source, target) in enumerate(((act_ref, act_buf), (up_ref, up_buf))):
            lanes = pl.ds(bunch * wide, wide)
            loads.append(
                pltpu.make_async_copy(
                    source.at[:, lanes], target.at[:, lanes], in_sems.at[bunch, which]
                )
            )
    small[0].start()
    for copy in loads[:AHEAD]:
        copy.start()
    small[1].start()
    small[2].start()
    small[0].wait()
    same = lax.broadcasted_iota(jnp.int32, (heads, heads), 0) == lax.broadcasted_iota(
        jnp.int32, (heads, heads), 1
    )
    scale = jnp.sum(jnp.where(same, scale_ref[...], 0.0), axis=1, keepdims=True)
    dt = dt_buf[...]
    log_decay = dt * scale
    across_ref[4 * heads :, :] = log_decay
    order = order_table(GROUP, True)
    stacked = jnp.concatenate([log_decay[:, b * GROUP : (b + 1) * GROUP] for b in range(blocks)], axis=0)
    running = exact_dot(stacked, order)
    totals = running[:, GROUP - 1 : GROUP]
    entering = jnp.exp(running)
    leaving = jnp.exp(totals - running)
    for block in range(blocks):
        span = slice(block * GROUP, (block + 1) * GROUP)
        some = slice(block * heads, (block + 1) * heads)
        across_ref[:heads, span] = running[some] * LOG2E
        across_ref[heads : 2 * heads, span] = running[some] * LOG2E - jnp.log2(dt[:, span])
        across_ref[2 * heads : 3 * heads, span] = leaving[some] * dt[:, span]
        across_ref[3 * heads : 4 * heads, span] = entering[some]
    small[3].start()
    first_total, second_total = totals[:heads], totals[heads:]
    first_running, second_running = running[:heads], running[heads:] + first_total
    device_total = first_total + second_total
    device_in = jnp.concatenate([entering[:heads], jnp.exp(second_running)], axis=1)
    device_out = dt * jnp.concatenate(
        [jnp.exp(device_total - first_running), leaving[heads:]], axis=1
    )
    columns = [jnp.exp(first_total), jnp.exp(second_total), jnp.exp(device_total)]
    table = channel_table(STEP, wide)
    table_low = table.astype(BF16)
    for bunch in range(bunches):
        lanes = slice(bunch * wide, (bunch + 1) * wide)
        some = slice(bunch * STEP, (bunch + 1) * STEP)
        first, second, both = (
            jnp.sum(table * column[some], axis=0, keepdims=True) for column in columns
        )
        spread_ref[:, lanes] = jnp.concatenate([first, second, both, jnp.zeros((5, wide), F32)], axis=0)
    small[4].start()
    small[1].wait()
    write_across = write_buf[...].T
    small[2].wait()
    read_across = read_buf[...].T
    per_pair = LANES // piece_rows
    stores = []
    for bunch in range(bunches):
        lanes = slice(bunch * wide, (bunch + 1) * wide)
        some = slice(bunch * STEP, (bunch + 1) * STEP)
        both = spread_ref[2:3, lanes]
        loads[2 * bunch].wait()
        if 2 * bunch + AHEAD < len(loads):
            loads[2 * bunch + AHEAD].start()
        act_scaled = act_buf[:, lanes].astype(F32) * spread_heads(device_out[some], table_low)
        state = dot_nn(write_across, act_scaled.astype(BF16))
        loads[2 * bunch + 1].wait()
        if 2 * bunch + 1 + AHEAD < len(loads):
            loads[2 * bunch + 1 + AHEAD].start()
        up_scaled = up_buf[:, lanes].astype(F32) * spread_heads(device_in[some], table_low)
        grad = dot_nn(read_across, up_scaled.astype(BF16))
        for local in range(STEP // 2):
            pair = bunch * STEP // 2 + local
            here = slice(local * LANES, (local + 1) * LANES)
            few = slice(pair * per_pair, (pair + 1) * per_pair)
            piece_buf[few, :piece_rows, :] = state[:, here].reshape(per_pair, piece_rows, LANES)
            piece_buf[few, piece_rows : 2 * piece_rows, :] = grad[:, here].reshape(
                per_pair, piece_rows, LANES
            )
            piece_buf[few, 2 * piece_rows :, :] = jnp.broadcast_to(
                both[:, here][None], (per_pair, 8, LANES)
            )
        few = pl.ds(bunch * STEP // 2 * per_pair, STEP // 2 * per_pair)
        copy = pltpu.make_async_copy(piece_buf.at[few], pieces_ref.at[few], out_sems.at[bunch])
        copy.start()
        stores.append(copy)
    for copy in stores + small[3:]:
        copy.wait()


def scan_kernel(piece_rows, got_ref, after_ref, carried_ref):
    count = got_ref.shape[0]
    zero = jnp.zeros((piece_rows, LANES), F32)

    def lap(step, carry):
        state, grad = carry
        carried_ref[step, :piece_rows, :] = state
        state = got_ref[step, 2 * piece_rows : 2 * piece_rows + 1, :] * state + got_ref[step, :piece_rows, :]
        back = count - 1 - step
        carried_ref[back, piece_rows:, :] = grad
        grad = (
            got_ref[back, piece_rows : 2 * piece_rows, :]
            + got_ref[back, 2 * piece_rows : 2 * piece_rows + 1, :] * grad
        )
        return state, grad

    lax.fori_loop(0, count, lap, (zero, zero), unroll=8)


def local_kernel(
    act_ref, up_ref, write_ref, read_ref, running_ref, shifted_ref, out_ref, in_ref,
    back_ref, act_scaled_ref, up_scaled_ref, inside_ref, write_part_ref, read_part_ref, done_ref,
    pair_sum, scores,
):
    bunch = pl.program_id(1)
    half = GROUP // 2
    wide = act_ref.shape[1]
    state = write_ref.shape[1]
    triangle = lax.broadcasted_iota(jnp.int32, (half, half), 0) <= lax.broadcasted_iota(
        jnp.int32, (half, half), 1
    )

    @pl.when(bunch == 0)
    def _():
        scores[...] = dot_nt(write_ref[...], read_ref[...])
        pair_sum[...] = jnp.zeros_like(pair_sum)

    table = channel_table(BUNCH, wide).astype(BF16)
    act_scaled = (act_ref[...].astype(F32) * spread_heads(out_ref[...], table)).astype(BF16)
    up_scaled = (up_ref[...].astype(F32) * spread_heads(in_ref[...], table)).astype(BF16)
    act_scaled_ref[...] = act_scaled.T
    up_scaled_ref[...] = up_scaled.T

    @pl.when(pl.program_id(0) == 0)
    def _():
        inside_ref[0, :state, :] = dot_tn(write_ref[...], act_scaled)

    @pl.when(pl.program_id(0) == 1)
    def _():
        inside_ref[0, :state, :] = dot_tn(read_ref[...], up_scaled)

    shifted = jnp.concatenate([shifted_ref[...], jnp.zeros((LANES - BUNCH, GROUP), F32)], axis=0).T
    left = left_half(GROUP)
    lane = lax.broadcasted_iota(jnp.int32, (GROUP, LANES), 1)
    columns = jnp.zeros((GROUP, LANES), F32)
    for pair in range(BUNCH // 2):
        here = slice(pair * LANES, (pair + 1) * LANES)
        act = act_ref[:, here]
        up = up_ref[:, here]
        back_top = jnp.zeros((half, LANES), F32)
        back_low = jnp.zeros((half, LANES), F32)
        for side in range(2):
            head = 2 * pair + side
            keep = left if side == 0 else jnp.logical_not(left)
            act_one = jnp.where(keep, act, jnp.zeros_like(act))
            up_one = jnp.where(keep, up, jnp.zeros_like(up))
            late = running_ref[head : head + 1, :]
            soon = shifted[:, head : head + 1]
            decay_a = jnp.where(triangle, jnp.exp2(late[:, :half] - soon[:half]), 0.0)
            decay_b = jnp.exp2(late[:, half:] - soon[:half])
            decay_c = jnp.where(triangle, jnp.exp2(late[:, half:] - soon[half:]), 0.0)
            decay_top = jnp.concatenate([decay_a, decay_b], axis=1)
            dots_top = dot_nt(act_one[:half], up)
            dots_low = dot_nt(act_one[half:], up[half:])
            pair_sum[:half, :] += decay_top * dots_top
            pair_sum[half:, half:] += decay_c * dots_low
            masked_top = (decay_top * scores[:half, :]).astype(BF16)
            masked_low = (decay_c * scores[half:, half:]).astype(BF16)
            sums = jnp.sum(masked_top.astype(F32) * dots_top, axis=0, keepdims=True)
            low_sums = jnp.sum(masked_low.astype(F32) * dots_low, axis=0, keepdims=True)
            inside_ref[0, state + head : state + head + 1, :half] = sums[:, :half]
            inside_ref[0, state + head : state + head + 1, half:GROUP] = sums[:, half:] + low_sums
            back_top += dot_nn(masked_top, up_one)
            back_low += dot_nn(masked_low, up_one[half:])
        back = jnp.concatenate([back_top, back_low], axis=0)
        back_ref[:, here] = back.astype(BF16)
        product = act.astype(F32) * back
        for side in range(2):
            keep = left if side == 0 else jnp.logical_not(left)
            one = jnp.sum(jnp.where(keep, product, 0.0), axis=1, keepdims=True)
            columns = jnp.where(lane == 2 * pair + side, one, columns)
    inside_ref[0, state + BUNCH :, :GROUP] = columns.T[:BUNCH]

    @pl.when(bunch == pl.num_programs(1) - 1)
    def _():
        low = pair_sum[...].astype(BF16)
        done_ref[...] = jnp.zeros_like(done_ref)
        write_part_ref[...] = dot_nn(low, read_ref[...])
        read_part_ref[...] = dot_tn(low, write_ref[...])


def cross_kernel(
    heads, piece_rows, act_scaled_ref, up_scaled_ref, back_ref, carried_ref, inside_ref, tables_ref, spread_ref,
    write_ref, read_ref, write_part_ref, read_part_ref,
    act_grad_ref, log_ref, write_grad_ref, read_grad_ref, act_grad_buf, read_acc, write_acc, read_buf, write_buf, sems, part_sems,
):
    inner, rows = act_scaled_ref.shape
    blocks = rows // GROUP
    bunches = heads // BUNCH
    channels = inner // heads
    state = write_ref.shape[1]
    parts = [
        pltpu.make_async_copy(source, target, part_sems.at[which])
        for which, (source, target) in enumerate(((write_part_ref, write_buf), (read_part_ref, read_buf)))
    ]
    for copy in parts:
        copy.start()
    wide = inner // bunches
    per_pair = LANES // piece_rows

    def gather(low, bunch):
        return jnp.concatenate(
            [
                carried_ref[pair * per_pair : (pair + 1) * per_pair, low : low + piece_rows, :].reshape(
                    LANES, LANES
                )
                for pair in range(bunch * wide // LANES, (bunch + 1) * wide // LANES)
            ],
            axis=1,
        )

    table = channel_table(BUNCH, wide)
    table_low = table.astype(BF16)
    write_across = [write_ref[b * GROUP : (b + 1) * GROUP, :].T for b in range(blocks)]
    read_across = [read_ref[b * GROUP : (b + 1) * GROUP, :].T for b in range(blocks)]

    def head_sums(product):
        return jnp.concatenate(
            [
                jnp.sum(product[h * channels : (h + 1) * channels], axis=0, keepdims=True)
                for h in range(BUNCH)
            ],
            axis=0,
        )

    order = order_table(GROUP, False)
    copies = []
    for bunch in range(bunches):
        if bunch == bunches - 1:
            for copy in parts:
                copy.wait()
        lanes = slice(bunch * wide, (bunch + 1) * wide)
        some = slice(bunch * BUNCH, (bunch + 1) * BUNCH)
        first, second = spread_ref[0:1, lanes], spread_ref[1:2, lanes]
        enter_0, leave_1 = gather(0, bunch), gather(piece_rows, bunch)
        kept_0, kept_1 = first * enter_0, second * leave_1
        enter_1 = kept_0 + inside_ref[0, :state, lanes]
        leave_0 = inside_ref[1, :state, lanes] + kept_1
        enters, leaves = (enter_0, enter_1), (leave_0, leave_1)
        edges = [
            jnp.sum(table * jnp.sum(product, axis=0, keepdims=True), axis=1, keepdims=True)
            for product in (leave_0 * kept_0, kept_1 * enter_1)
        ]
        nets, cols = [], []
        for block in range(blocks):
            span = slice(block * GROUP, (block + 1) * GROUP)
            enter_low = enters[block].astype(BF16)
            leave_low = leaves[block].astype(BF16)
            cross = dot_nn(write_ref[span, :], leave_low)
            decay_out = spread_heads(tables_ref[2 * heads + bunch * BUNCH : 2 * heads + (bunch + 1) * BUNCH, span], table_low)
            act_grad_buf[span, lanes] = (back_ref[span, lanes].astype(F32) + decay_out * cross).astype(BF16)
            act_scaled, up_scaled = act_scaled_ref[lanes, span], up_scaled_ref[lanes, span]
            row_sums = head_sums(dot_tn(enter_low, read_across[block]) * up_scaled.astype(F32))
            col_sums = head_sums(dot_tn(leave_low, write_across[block]) * act_scaled.astype(F32))
            near = slice(bunch * wide, bunch * wide + GROUP)
            column = inside_ref[block, state + BUNCH :, near] + col_sums
            nets.append(inside_ref[block, state : state + BUNCH, near] + row_sums - column)
            cols.append(column)
            edges[block] += jnp.sum(col_sums, axis=1, keepdims=True)
            read_cross = dot_nn(enter_low, up_scaled)
            write_cross = dot_nn(leave_low, act_scaled)
            if bunch == 0:
                read_acc[:, span] = read_cross
                write_acc[:, span] = write_cross
            elif bunch < bunches - 1:
                read_acc[:, span] += read_cross
                write_acc[:, span] += write_cross
            else:
                read_buf[span, :] += (read_acc[:, span] + read_cross).T
                write_buf[span, :] += (write_acc[:, span] + write_cross).T
        few = pl.ds(bunch * wide, wide)
        copy = pltpu.make_async_copy(act_grad_buf.at[:, few], act_grad_ref.at[:, few], sems.at[bunch])
        copy.start()
        copies.append(copy)
        suffix = exact_dot(jnp.concatenate(nets, axis=0), order)
        for block in range(blocks):
            span = slice(block * GROUP, (block + 1) * GROUP)
            log_grad = suffix[block * BUNCH : (block + 1) * BUNCH] + edges[block]
            log_ref[some, span] = cols[block] + tables_ref[4 * heads + bunch * BUNCH : 4 * heads + (bunch + 1) * BUNCH, span] * log_grad
    for which, (source, target) in enumerate(((write_buf, write_grad_ref), (read_buf, read_grad_ref))):
        copy = pltpu.make_async_copy(source, target, part_sems.at[2 + which])
        copy.start()
        copies.append(copy)
    for copy in copies:
        copy.wait()


def on_device(activation, step_size, decay_scale, write_vectors, read_vectors, upstream):
    rows, inner = activation.shape
    heads = decay_scale.shape[0]
    state = write_vectors.shape[1]
    count = lax.axis_size("seq")
    pairs = heads // 2
    piece_rows = pairs * state // count
    bunches = heads // BUNCH
    blocks = rows // GROUP
    wide = inner // bunches
    scale = decay_scale.reshape(1, heads)
    vmem = pl.BlockSpec(memory_space=pltpu.VMEM)
    hbm = pl.BlockSpec(memory_space=pl.ANY)
    across = jax.ShapeDtypeStruct((heads, rows), F32)
    low = jax.ShapeDtypeStruct((rows, inner), BF16)
    low_across = jax.ShapeDtypeStruct((inner, rows), BF16)
    part = jax.ShapeDtypeStruct((rows, state), F32)

    pieces, tables, spread = pl.pallas_call(
        partial(states_kernel, heads, piece_rows),
        name="states",
        in_specs=[hbm, vmem] + [hbm] * 4,
        out_specs=[hbm] * 3,
        out_shape=[
            jax.ShapeDtypeStruct((count, 2 * piece_rows + 8, LANES), F32),
            jax.ShapeDtypeStruct((5 * heads, rows), F32),
            jax.ShapeDtypeStruct((8, inner), F32),
        ],
        scratch_shapes=[
            pltpu.VMEM((heads, rows), F32),
            pltpu.VMEM((rows, state), BF16),
            pltpu.VMEM((rows, state), BF16),
            pltpu.VMEM((rows, inner), BF16),
            pltpu.VMEM((rows, inner), BF16),
            pltpu.VMEM((count, 2 * piece_rows + 8, LANES), F32),
            pltpu.VMEM((5 * heads, rows), F32),
            pltpu.VMEM((8, inner), F32),
            pltpu.SemaphoreType.DMA((heads // STEP, 2)),
            pltpu.SemaphoreType.DMA((5,)),
            pltpu.SemaphoreType.DMA((heads // STEP,)),
        ],
        compiler_params=pltpu.CompilerParams(vmem_limit_bytes=VMEM_LIMIT),
        cost_estimate=pl.CostEstimate(flops=4 * rows * state * inner, bytes_accessed=8 * MIB, transcendentals=0),
    )(step_size.T, scale, write_vectors, read_vectors, activation, upstream)

    got = lax.all_to_all(pieces, "seq", 0, 0)

    def table(which):
        return pl.BlockSpec((BUNCH, GROUP), lambda b, g: (which * bunches + g, b))

    block_wide = pl.BlockSpec((GROUP, wide), lambda b, g: (b, g))
    block_tall = pl.BlockSpec((wide, GROUP), lambda b, g: (g, b))
    block_state = pl.BlockSpec((GROUP, state), lambda b, g: (b, 0))
    back, act_scaled, up_scaled, inside, write_part, read_part, done = pl.pallas_call(
        local_kernel,
        name="local",
        grid=(blocks, bunches),
        in_specs=[block_wide, block_wide, block_state, block_state] + [table(i) for i in range(4)],
        out_specs=[
            block_wide,
            block_tall,
            block_tall,
            pl.BlockSpec((1, state + 2 * BUNCH, wide), lambda b, g: (b, 0, g)),
            block_state,
            block_state,
            pl.BlockSpec((8, LANES), lambda b, g: (0, 0)),
        ],
        out_shape=[low, low_across, low_across, jax.ShapeDtypeStruct((blocks, state + 2 * BUNCH, inner), F32), part, part, jax.ShapeDtypeStruct((8, LANES), F32)],
        scratch_shapes=[pltpu.VMEM((GROUP, GROUP), F32), pltpu.VMEM((GROUP, GROUP), F32)],
        compiler_params=pltpu.CompilerParams(vmem_limit_bytes=56 * MIB),
        cost_estimate=pl.CostEstimate(
            flops=20_000_000_000, bytes_accessed=8 * MIB, transcendentals=blocks * heads * GROUP * GROUP
        ),
    )(activation, upstream, write_vectors, read_vectors, tables, tables, tables, tables)

    carried = pl.pallas_call(
        partial(scan_kernel, piece_rows),
        name="scan",
        in_specs=[vmem, pl.BlockSpec(memory_space=pltpu.HBM)],
        out_specs=vmem,
        out_shape=jax.ShapeDtypeStruct((count, 2 * piece_rows, LANES), F32),
        compiler_params=pltpu.CompilerParams(vmem_limit_bytes=8 * MIB),
    )(got, done)
    carried = lax.all_to_all(carried, "seq", 0, 0)

    act_grad, log_grad, write_grad, read_grad = pl.pallas_call(
        partial(cross_kernel, heads, piece_rows),
        name="cross",
        in_specs=[vmem] * 9 + [hbm] * 2,
        out_specs=[hbm, vmem, hbm, hbm],
        input_output_aliases={9: 2, 10: 3},
        out_shape=[low, across, part, part],
        scratch_shapes=[
            pltpu.VMEM((rows, inner), BF16),
            pltpu.VMEM((state, rows), F32),
            pltpu.VMEM((state, rows), F32),
            pltpu.VMEM((rows, state), F32),
            pltpu.VMEM((rows, state), F32),
            pltpu.SemaphoreType.DMA((bunches,)),
            pltpu.SemaphoreType.DMA((4,)),
        ],
        compiler_params=pltpu.CompilerParams(vmem_limit_bytes=16 * MIB),
        cost_estimate=pl.CostEstimate(flops=8 * rows * state * inner, bytes_accessed=16 * MIB, transcendentals=0),
    )(
        act_scaled, up_scaled, back, carried, inside, tables, spread,
        write_vectors, read_vectors, write_part, read_part,
    )
    return act_grad, log_grad.T, write_grad, read_grad


def solution(mesh):
    spread = P(("dp", "seq"), None)
    return jax.shard_map(
        on_device,
        mesh=mesh,
        in_specs=(spread, spread, P("dp"), spread, spread, spread),
        out_specs=(spread, spread, spread, spread),
        check_vma=False,
    )
```

```python
import math
from functools import partial

import jax
import jax.numpy as jnp
from jax import lax
from jax.experimental import pallas as pl
from jax.experimental.pallas import tpu as pltpu
from jax.sharding import PartitionSpec as P

GROUP = 256
LANES = 128
BUNCH = 8
LOG2E = math.log2(math.e)
F32 = jnp.float32
BF16 = jnp.bfloat16
MIB = 1 << 20
VMEM_LIMIT = 56 * MIB
AHEAD = 2
STEP = 16


def dot_nn(a, b):
    return jnp.dot(a, b, preferred_element_type=F32)


def dot_nt(a, b):
    return lax.dot_general(a, b, (((1,), (1,)), ((), ())), preferred_element_type=F32)


def dot_tn(a, b):
    return lax.dot_general(a, b, (((0,), (0,)), ((), ())), preferred_element_type=F32)


def split(value, terms):
    parts = []
    for _ in range(terms):
        part = value.astype(BF16)
        parts.append(part)
        value = value - part.astype(F32)
    return jnp.concatenate(parts, axis=0)


def exact_dot(value, table):
    rows = value.shape[0]
    product = dot_nn(split(value, 3), table)
    return product[:rows] + product[rows : 2 * rows] + product[2 * rows :]


def left_half(rows):
    return lax.broadcasted_iota(jnp.int32, (rows, LANES), 1) < LANES // 2


def order_table(size, upper):
    row = lax.broadcasted_iota(jnp.int32, (size, size), 0)
    column = lax.broadcasted_iota(jnp.int32, (size, size), 1)
    return jnp.where(row <= column if upper else row >= column, 1.0, 0.0).astype(BF16)


def channel_table(heads, width):
    head = lax.broadcasted_iota(jnp.int32, (heads, width), 0)
    lane = lax.broadcasted_iota(jnp.int32, (heads, width), 1)
    return jnp.where(lane // (width // heads) == head, 1.0, 0.0)


def spread_heads(across, table):
    return dot_tn(split(across, 2), jnp.concatenate([table, table], axis=0))


def states_kernel(
    heads, piece_rows, dt_ref, scale_ref, write_ref, read_ref, act_ref, up_ref,
    pieces_ref, tables_ref, spread_hbm_ref, dt_buf, write_buf, read_buf, act_buf, up_buf, piece_buf, across_ref, spread_ref,
    in_sems, small_sems, out_sems,
):
    rows = dt_ref.shape[1]
    blocks = rows // GROUP
    bunches = heads // STEP
    wide = STEP // 2 * LANES
    small = [
        pltpu.make_async_copy(source, target, small_sems.at[which])
        for which, (source, target) in enumerate(
            ((dt_ref, dt_buf), (write_ref, write_buf), (read_ref, read_buf), (across_ref, tables_ref), (spread_ref, spread_hbm_ref))
        )
    ]
    loads = []
    for bunch in range(bunches):
        for which, (source, target) in enumerate(((act_ref, act_buf), (up_ref, up_buf))):
            lanes = pl.ds(bunch * wide, wide)
            loads.append(
                pltpu.make_async_copy(
                    source.at[:, lanes], target.at[:, lanes], in_sems.at[bunch, which]
                )
            )
    small[0].start()
    for copy in loads[:AHEAD]:
        copy.start()
    small[1].start()
    small[2].start()
    small[0].wait()
    same = lax.broadcasted_iota(jnp.int32, (heads, heads), 0) == lax.broadcasted_iota(
        jnp.int32, (heads, heads), 1
    )
    scale = jnp.sum(jnp.where(same, scale_ref[...], 0.0), axis=1, keepdims=True)
    dt = dt_buf[...]
    log_decay = dt * scale
    across_ref[4 * heads :, :] = log_decay
    order = order_table(GROUP, True)
    stacked = jnp.concatenate([log_decay[:, b * GROUP : (b + 1) * GROUP] for b in range(blocks)], axis=0)
    running = exact_dot(stacked, order)
    totals = running[:, GROUP - 1 : GROUP]
    entering = jnp.exp(running)
    leaving = jnp.exp(totals - running)
    for block in range(blocks):
        span = slice(block * GROUP, (block + 1) * GROUP)
        some = slice(block * heads, (block + 1) * heads)
        across_ref[:heads, span] = running[some] * LOG2E
        across_ref[heads : 2 * heads, span] = running[some] * LOG2E - jnp.log2(dt[:, span])
        across_ref[2 * heads : 3 * heads, span] = leaving[some] * dt[:, span]
        across_ref[3 * heads : 4 * heads, span] = entering[some]
    small[3].start()
    first_total, second_total = totals[:heads], totals[heads:]
    first_running, second_running = running[:heads], running[heads:] + first_total
    device_total = first_total + second_total
    device_in = jnp.concatenate([entering[:heads], jnp.exp(second_running)], axis=1)
    device_out = dt * jnp.concatenate(
        [jnp.exp(device_total - first_running), leaving[heads:]], axis=1
    )
    columns = [jnp.exp(first_total), jnp.exp(second_total), jnp.exp(device_total)]
    table = channel_table(STEP, wide)
    table_low = table.astype(BF16)
    for bunch in range(bunches):
        lanes = slice(bunch * wide, (bunch + 1) * wide)
        some = slice(bunch * STEP, (bunch + 1) * STEP)
        first, second, both = (
            jnp.sum(table * column[some], axis=0, keepdims=True) for column in columns
        )
        spread_ref[:, lanes] = jnp.concatenate([first, second, both, jnp.zeros((5, wide), F32)], axis=0)
    small[4].start()
    small[1].wait()
    write_across = write_buf[...].T
    small[2].wait()
    read_across = read_buf[...].T
    per_pair = LANES // piece_rows
    stores = []
    for bunch in range(bunches):
        lanes = slice(bunch * wide, (bunch + 1) * wide)
        some = slice(bunch * STEP, (bunch + 1) * STEP)
        both = spread_ref[2:3, lanes]
        loads[2 * bunch].wait()
        if 2 * bunch + AHEAD < len(loads):
            loads[2 * bunch + AHEAD].start()
        act_scaled = act_buf[:, lanes].astype(F32) * spread_heads(device_out[some], table_low)
        state = dot_nn(write_across, act_scaled.astype(BF16))
        loads[2 * bunch + 1].wait()
        if 2 * bunch + 1 + AHEAD < len(loads):
            loads[2 * bunch + 1 + AHEAD].start()
        up_scaled = up_buf[:, lanes].astype(F32) * spread_heads(device_in[some], table_low)
        grad = dot_nn(read_across, up_scaled.astype(BF16))
        for local in range(STEP // 2):
            pair = bunch * STEP // 2 + local
            here = slice(local * LANES, (local + 1) * LANES)
            few = slice(pair * per_pair, (pair + 1) * per_pair)
            piece_buf[few, :piece_rows, :] = state[:, here].reshape(per_pair, piece_rows, LANES)
            piece_buf[few, piece_rows : 2 * piece_rows, :] = grad[:, here].reshape(
                per_pair, piece_rows, LANES
            )
            piece_buf[few, 2 * piece_rows :, :] = jnp.broadcast_to(
                both[:, here][None], (per_pair, 8, LANES)
            )
        few = pl.ds(bunch * STEP // 2 * per_pair, STEP // 2 * per_pair)
        copy = pltpu.make_async_copy(piece_buf.at[few], pieces_ref.at[few], out_sems.at[bunch])
        copy.start()
        stores.append(copy)
    for copy in stores + small[3:]:
        copy.wait()


def scan_kernel(piece_rows, got_ref, after_ref, carried_ref):
    count = got_ref.shape[0]
    zero = jnp.zeros((piece_rows, LANES), F32)

    def lap(step, carry):
        state, grad = carry
        carried_ref[step, :piece_rows, :] = state
        state = got_ref[step, 2 * piece_rows : 2 * piece_rows + 1, :] * state + got_ref[step, :piece_rows, :]
        back = count - 1 - step
        carried_ref[back, piece_rows:, :] = grad
        grad = (
            got_ref[back, piece_rows : 2 * piece_rows, :]
            + got_ref[back, 2 * piece_rows : 2 * piece_rows + 1, :] * grad
        )
        return state, grad

    lax.fori_loop(0, count, lap, (zero, zero), unroll=8)


def local_kernel(
    act_ref, up_ref, write_ref, read_ref, running_ref, shifted_ref, out_ref, in_ref,
    back_ref, act_scaled_ref, up_scaled_ref, inside_ref, write_part_ref, read_part_ref, done_ref,
    pair_sum, scores,
):
    bunch = pl.program_id(1)
    half = GROUP // 2
    wide = act_ref.shape[1]
    state = write_ref.shape[1]
    triangle = lax.broadcasted_iota(jnp.int32, (half, half), 0) <= lax.broadcasted_iota(
        jnp.int32, (half, half), 1
    )

    @pl.when(bunch == 0)
    def _():
        scores[...] = dot_nt(write_ref[...], read_ref[...])
        pair_sum[...] = jnp.zeros_like(pair_sum)

    table = channel_table(BUNCH, wide).astype(BF16)
    act_scaled = (act_ref[...].astype(F32) * spread_heads(out_ref[...], table)).astype(BF16)
    up_scaled = (up_ref[...].astype(F32) * spread_heads(in_ref[...], table)).astype(BF16)
    act_scaled_ref[...] = act_scaled.T
    up_scaled_ref[...] = up_scaled.T

    @pl.when(pl.program_id(0) == 0)
    def _():
        inside_ref[0, :state, :] = dot_tn(write_ref[...], act_scaled)

    @pl.when(pl.program_id(0) == 1)
    def _():
        inside_ref[0, :state, :] = dot_tn(read_ref[...], up_scaled)

    shifted = jnp.concatenate([shifted_ref[...], jnp.zeros((LANES - BUNCH, GROUP), F32)], axis=0).T
    left = left_half(GROUP)
    lane = lax.broadcasted_iota(jnp.int32, (GROUP, LANES), 1)
    columns = jnp.zeros((GROUP, LANES), F32)
    for pair in range(BUNCH // 2):
        here = slice(pair * LANES, (pair + 1) * LANES)
        act = act_ref[:, here]
        up = up_ref[:, here]
        back_top = jnp.zeros((half, LANES), F32)
        back_low = jnp.zeros((half, LANES), F32)
        for side in range(2):
            head = 2 * pair + side
            keep = left if side == 0 else jnp.logical_not(left)
            act_one = jnp.where(keep, act, jnp.zeros_like(act))
            up_one = jnp.where(keep, up, jnp.zeros_like(up))
            late = running_ref[head : head + 1, :]
            soon = shifted[:, head : head + 1]
            decay_a = jnp.where(triangle, jnp.exp2(late[:, :half] - soon[:half]), 0.0)
            decay_b = jnp.exp2(late[:, half:] - soon[:half])
            decay_c = jnp.where(triangle, jnp.exp2(late[:, half:] - soon[half:]), 0.0)
            decay_top = jnp.concatenate([decay_a, decay_b], axis=1)
            dots_top = dot_nt(act_one[:half], up)
            dots_low = dot_nt(act_one[half:], up[half:])
            pair_sum[:half, :] += decay_top * dots_top
            pair_sum[half:, half:] += decay_c * dots_low
            masked_top = (decay_top * scores[:half, :]).astype(BF16)
            masked_low = (decay_c * scores[half:, half:]).astype(BF16)
            sums = jnp.sum(masked_top.astype(F32) * dots_top, axis=0, keepdims=True)
            low_sums = jnp.sum(masked_low.astype(F32) * dots_low, axis=0, keepdims=True)
            inside_ref[0, state + head : state + head + 1, :half] = sums[:, :half]
            inside_ref[0, state + head : state + head + 1, half:GROUP] = sums[:, half:] + low_sums
            back_top += dot_nn(masked_top, up_one)
            back_low += dot_nn(masked_low, up_one[half:])
        back = jnp.concatenate([back_top, back_low], axis=0)
        back_ref[:, here] = back.astype(BF16)
        product = act.astype(F32) * back
        for side in range(2):
            keep = left if side == 0 else jnp.logical_not(left)
            one = jnp.sum(jnp.where(keep, product, 0.0), axis=1, keepdims=True)
            columns = jnp.where(lane == 2 * pair + side, one, columns)
    inside_ref[0, state + BUNCH :, :GROUP] = columns.T[:BUNCH]

    @pl.when(bunch == pl.num_programs(1) - 1)
    def _():
        low = pair_sum[...].astype(BF16)
        done_ref[...] = jnp.zeros_like(done_ref)
        write_part_ref[...] = dot_nn(low, read_ref[...])
        read_part_ref[...] = dot_tn(low, write_ref[...])


def cross_kernel(
    heads, piece_rows, act_scaled_ref, up_scaled_ref, back_ref, carried_ref, inside_ref, tables_ref, spread_ref,
    write_ref, read_ref, write_part_ref, read_part_ref,
    act_grad_ref, log_ref, write_grad_ref, read_grad_ref, act_grad_buf, read_acc, write_acc, read_buf, write_buf, sems, part_sems,
):
    inner, rows = act_scaled_ref.shape
    blocks = rows // GROUP
    bunches = heads // BUNCH
    channels = inner // heads
    state = write_ref.shape[1]
    parts = [
        pltpu.make_async_copy(source, target, part_sems.at[which])
        for which, (source, target) in enumerate(((write_part_ref, write_buf), (read_part_ref, read_buf)))
    ]
    for copy in parts:
        copy.start()
    wide = inner // bunches
    per_pair = LANES // piece_rows

    def gather(low, bunch):
        return jnp.concatenate(
            [
                carried_ref[pair * per_pair : (pair + 1) * per_pair, low : low + piece_rows, :].reshape(
                    LANES, LANES
                )
                for pair in range(bunch * wide // LANES, (bunch + 1) * wide // LANES)
            ],
            axis=1,
        )

    table = channel_table(BUNCH, wide)
    table_low = table.astype(BF16)
    write_across = [write_ref[b * GROUP : (b + 1) * GROUP, :].T for b in range(blocks)]
    read_across = [read_ref[b * GROUP : (b + 1) * GROUP, :].T for b in range(blocks)]

    def head_sums(product):
        return jnp.concatenate(
            [
                jnp.sum(product[h * channels : (h + 1) * channels], axis=0, keepdims=True)
                for h in range(BUNCH)
            ],
            axis=0,
        )

    order = order_table(GROUP, False)
    copies = []
    for bunch in range(bunches):
        if bunch == bunches - 1:
            for copy in parts:
                copy.wait()
        lanes = slice(bunch * wide, (bunch + 1) * wide)
        some = slice(bunch * BUNCH, (bunch + 1) * BUNCH)
        first, second = spread_ref[0:1, lanes], spread_ref[1:2, lanes]
        enter_0, leave_1 = gather(0, bunch), gather(piece_rows, bunch)
        kept_0, kept_1 = first * enter_0, second * leave_1
        enter_1 = kept_0 + inside_ref[0, :state, lanes]
        leave_0 = inside_ref[1, :state, lanes] + kept_1
        enters, leaves = (enter_0, enter_1), (leave_0, leave_1)
        edges = [
            jnp.sum(table * jnp.sum(product, axis=0, keepdims=True), axis=1, keepdims=True)
            for product in (leave_0 * kept_0, kept_1 * enter_1)
        ]
        nets, cols = [], []
        for block in range(blocks):
            span = slice(block * GROUP, (block + 1) * GROUP)
            enter_low = enters[block].astype(BF16)
            leave_low = leaves[block].astype(BF16)
            cross = dot_nn(write_ref[span, :], leave_low)
            decay_out = spread_heads(tables_ref[2 * heads + bunch * BUNCH : 2 * heads + (bunch + 1) * BUNCH, span], table_low)
            act_grad_buf[span, lanes] = (back_ref[span, lanes].astype(F32) + decay_out * cross).astype(BF16)
            act_scaled, up_scaled = act_scaled_ref[lanes, span], up_scaled_ref[lanes, span]
            row_sums = head_sums(dot_tn(enter_low, read_across[block]) * up_scaled.astype(F32))
            col_sums = head_sums(dot_tn(leave_low, write_across[block]) * act_scaled.astype(F32))
            near = slice(bunch * wide, bunch * wide + GROUP)
            column = inside_ref[block, state + BUNCH :, near] + col_sums
            nets.append(inside_ref[block, state : state + BUNCH, near] + row_sums - column)
            cols.append(column)
            edges[block] += jnp.sum(col_sums, axis=1, keepdims=True)
            read_cross = dot_nn(enter_low, up_scaled)
            write_cross = dot_nn(leave_low, act_scaled)
            if bunch == 0:
                read_acc[:, span] = read_cross
                write_acc[:, span] = write_cross
            elif bunch < bunches - 1:
                read_acc[:, span] += read_cross
                write_acc[:, span] += write_cross
            else:
                read_buf[span, :] += (read_acc[:, span] + read_cross).T
                write_buf[span, :] += (write_acc[:, span] + write_cross).T
        few = pl.ds(bunch * wide, wide)
        copy = pltpu.make_async_copy(act_grad_buf.at[:, few], act_grad_ref.at[:, few], sems.at[bunch])
        copy.start()
        copies.append(copy)
        suffix = exact_dot(jnp.concatenate(nets, axis=0), order)
        for block in range(blocks):
            span = slice(block * GROUP, (block + 1) * GROUP)
            log_grad = suffix[block * BUNCH : (block + 1) * BUNCH] + edges[block]
            log_ref[some, span] = cols[block] + tables_ref[4 * heads + bunch * BUNCH : 4 * heads + (bunch + 1) * BUNCH, span] * log_grad
    for which, (source, target) in enumerate(((write_buf, write_grad_ref), (read_buf, read_grad_ref))):
        copy = pltpu.make_async_copy(source, target, part_sems.at[2 + which])
        copy.start()
        copies.append(copy)
    for copy in copies:
        copy.wait()


def on_device(activation, step_size, decay_scale, write_vectors, read_vectors, upstream):
    rows, inner = activation.shape
    heads = decay_scale.shape[0]
    state = write_vectors.shape[1]
    count = lax.axis_size("seq")
    pairs = heads // 2
    piece_rows = pairs * state // count
    bunches = heads // BUNCH
    blocks = rows // GROUP
    wide = inner // bunches
    scale = decay_scale.reshape(1, heads)
    vmem = pl.BlockSpec(memory_space=pltpu.VMEM)
    hbm = pl.BlockSpec(memory_space=pl.ANY)
    across = jax.ShapeDtypeStruct((heads, rows), F32)
    low = jax.ShapeDtypeStruct((rows, inner), BF16)
    low_across = jax.ShapeDtypeStruct((inner, rows), BF16)
    part = jax.ShapeDtypeStruct((rows, state), F32)

    pieces, tables, spread = pl.pallas_call(
        partial(states_kernel, heads, piece_rows),
        name="states",
        in_specs=[hbm, vmem] + [hbm] * 4,
        out_specs=[hbm] * 3,
        out_shape=[
            jax.ShapeDtypeStruct((count, 2 * piece_rows + 8, LANES), F32),
            jax.ShapeDtypeStruct((5 * heads, rows), F32),
            jax.ShapeDtypeStruct((8, inner), F32),
        ],
        scratch_shapes=[
            pltpu.VMEM((heads, rows), F32),
            pltpu.VMEM((rows, state), BF16),
            pltpu.VMEM((rows, state), BF16),
            pltpu.VMEM((rows, inner), BF16),
            pltpu.VMEM((rows, inner), BF16),
            pltpu.VMEM((count, 2 * piece_rows + 8, LANES), F32),
            pltpu.VMEM((5 * heads, rows), F32),
            pltpu.VMEM((8, inner), F32),
            pltpu.SemaphoreType.DMA((heads // STEP, 2)),
            pltpu.SemaphoreType.DMA((5,)),
            pltpu.SemaphoreType.DMA((heads // STEP,)),
        ],
        compiler_params=pltpu.CompilerParams(vmem_limit_bytes=VMEM_LIMIT),
        cost_estimate=pl.CostEstimate(flops=4 * rows * state * inner, bytes_accessed=8 * MIB, transcendentals=0),
    )(step_size.T, scale, write_vectors, read_vectors, activation, upstream)

    got = lax.all_to_all(pieces, "seq", 0, 0)

    def table(which):
        return pl.BlockSpec((BUNCH, GROUP), lambda b, g: (which * bunches + g, b))

    block_wide = pl.BlockSpec((GROUP, wide), lambda b, g: (b, g))
    block_tall = pl.BlockSpec((wide, GROUP), lambda b, g: (g, b))
    block_state = pl.BlockSpec((GROUP, state), lambda b, g: (b, 0))
    back, act_scaled, up_scaled, inside, write_part, read_part, done = pl.pallas_call(
        local_kernel,
        name="local",
        grid=(blocks, bunches),
        in_specs=[block_wide, block_wide, block_state, block_state] + [table(i) for i in range(4)],
        out_specs=[
            block_wide,
            block_tall,
            block_tall,
            pl.BlockSpec((1, state + 2 * BUNCH, wide), lambda b, g: (b, 0, g)),
            block_state,
            block_state,
            pl.BlockSpec((8, LANES), lambda b, g: (0, 0)),
        ],
        out_shape=[low, low_across, low_across, jax.ShapeDtypeStruct((blocks, state + 2 * BUNCH, inner), F32), part, part, jax.ShapeDtypeStruct((8, LANES), F32)],
        scratch_shapes=[pltpu.VMEM((GROUP, GROUP), F32), pltpu.VMEM((GROUP, GROUP), F32)],
        compiler_params=pltpu.CompilerParams(vmem_limit_bytes=53 * MIB),
        cost_estimate=pl.CostEstimate(
            flops=20_000_000_000, bytes_accessed=8 * MIB, transcendentals=blocks * heads * GROUP * GROUP
        ),
    )(activation, upstream, write_vectors, read_vectors, tables, tables, tables, tables)

    carried = pl.pallas_call(
        partial(scan_kernel, piece_rows),
        name="scan",
        in_specs=[vmem, pl.BlockSpec(memory_space=pltpu.HBM)],
        out_specs=vmem,
        out_shape=jax.ShapeDtypeStruct((count, 2 * piece_rows, LANES), F32),
        compiler_params=pltpu.CompilerParams(vmem_limit_bytes=8 * MIB),
    )(got, done)
    carried = lax.all_to_all(carried, "seq", 0, 0)

    act_grad, log_grad, write_grad, read_grad = pl.pallas_call(
        partial(cross_kernel, heads, piece_rows),
        name="cross",
        in_specs=[vmem] * 9 + [hbm] * 2,
        out_specs=[hbm, vmem, hbm, hbm],
        input_output_aliases={9: 2, 10: 3},
        out_shape=[low, across, part, part],
        scratch_shapes=[
            pltpu.VMEM((rows, inner), BF16),
            pltpu.VMEM((state, rows), F32),
            pltpu.VMEM((state, rows), F32),
            pltpu.VMEM((rows, state), F32),
            pltpu.VMEM((rows, state), F32),
            pltpu.SemaphoreType.DMA((bunches,)),
            pltpu.SemaphoreType.DMA((4,)),
        ],
        compiler_params=pltpu.CompilerParams(vmem_limit_bytes=16 * MIB),
        cost_estimate=pl.CostEstimate(flops=8 * rows * state * inner, bytes_accessed=16 * MIB, transcendentals=0),
    )(
        act_scaled, up_scaled, back, carried, inside, tables, spread,
        write_vectors, read_vectors, write_part, read_part,
    )
    return act_grad, log_grad.T, write_grad, read_grad


def solution(mesh):
    spread = P(("dp", "seq"), None)
    return jax.shard_map(
        on_device,
        mesh=mesh,
        in_specs=(spread, spread, P("dp"), spread, spread, spread),
        out_specs=(spread, spread, spread, spread),
        check_vma=False,
    )
```
